256 devices in a mesh: req: 64 (over y, z_hi, x, core), head: 4 (over z_lo).
Axes of the slice: x: 4, y: 4, z: 8 (z_hi: 2, z_lo: 4; z = z_hi * 4 + z_lo), core: 2. Of those that a mesh axis runs over, the one named last changes fastest.
Arguments:
- kv_cache: bfloat16 [512, 4, 512, 192], P('req', 'head'), may hold values from -6 to 6
- first_fresh: bfloat16 [512, 4, 192], P('req', 'head'), may hold values from -6 to 6
- second_fresh: bfloat16 [512, 4, 192], P('req', 'head'), may hold values from -6 to 6
- first_query: bfloat16 [512, 4, 1024], P('req', 'head'), may hold values from -272 to 272
- second_query: bfloat16 [512, 4, 1024], P('req', 'head'), may hold values from -272 to 272
- key_basis: bfloat16 [4, 64, 128], P('head'), may hold values from -0.75 to 0.75
- out_weight: bfloat16 [4096, 4096], P('head'), may hold values from -1.5 to 1.5
- lengths: int32 [64, 8], replicated, may hold values from 128 to 384, as said below
- leave_slot: int32 [64, 4], replicated, may hold values from 0 to 7, as said below
- arrive_row: int32 [64, 4], replicated, may hold values from 0 to 511, as said below
Outputs:
- first_out: bfloat16 [512, 4096], P('req', 'head')
- second_out: bfloat16 [512, 4096], P('req', 'head')
- final_cache: bfloat16 [512, 4, 512, 192], P('req', 'head')
The draws below stay inside these ranges and needn't reach their ends.
Inputs may be any that keep to these rules, and one draw needn't show every extreme that they name: `lengths`: A multiple of 128; in every group some row has exactly 384 tokens. `leave_slot`: the 4 slots of a group are distinct. `arrive_row`: the targets are exactly the rows that are left, each once; no group sends two rows to the same group.
All inputs are finite; a program needn't handle non-finite values.
Results may differ from the reference program's by a relative error of at most 0.015.
The reference program's roundings to bfloat16 on the way (of `first_cache`, `reduced`, `weights`, `attended` and `moved_cache`) count: a program that leaves them out, or rounds other values in their place, can miss the bound.
Values may be sent and summed in bfloat16 or wider, within the bound.
A program may use at most 128 MiB of HBM per device.

```python
import math
import jax
import jax.numpy as jnp
from jax import lax

D = 4096
HD = 128
RANK = 64
QPK = 8
ROWS = 8
MIG = 4
LMAX = 512
KV_HEADS = 4
ENTRY = 192
GROUPS = 64
N_REQ = 64
N_HEAD = 4


def plan_tables(key):
    key = jax.random.fold_in(key, 11)
    keys = jax.random.split(key, 5)
    leaving = jax.vmap(lambda sub: jax.random.permutation(sub, ROWS)[:MIG])(jax.random.split(keys[0], N_REQ)).astype(jnp.int32)
    outer_perm = jax.random.permutation(keys[1], N_REQ).astype(jnp.int32)
    inner_perm = jax.random.permutation(keys[2], N_REQ).astype(jnp.int32)
    offsets = jax.random.permutation(keys[3], N_REQ)[:MIG].astype(jnp.int32)
    group_ids = jnp.arange(N_REQ, dtype=jnp.int32)
    dest_group = outer_perm[(inner_perm[group_ids][:, None] + offsets[None, :]) % N_REQ]
    layer_perm = jax.vmap(lambda sub: jax.random.permutation(sub, MIG))(jax.random.split(keys[4], N_REQ)).astype(jnp.int32)
    layer_ids = jnp.broadcast_to(jnp.arange(MIG, dtype=jnp.int32)[None, :], (N_REQ, MIG))
    slot_pick = layer_perm[dest_group, layer_ids]
    arriving = dest_group * ROWS + leaving[dest_group, slot_pick]
    return (leaving, arriving.astype(jnp.int32))


def draw_leave_slot(key, part):
    return plan_tables(key)[0]


def draw_arrive_row(key, part):
    return plan_tables(key)[1]


def draw_lengths(key, part):
    key = jax.random.fold_in(key, 3)
    first_key, second_key = jax.random.split(key)
    base = 128 * jax.random.randint(first_key, (N_REQ, ROWS), 1, LMAX // 128)
    longest = jax.random.randint(second_key, (N_REQ,), 0, ROWS)
    slot_ids = jnp.arange(ROWS, dtype=jnp.int32)[None, :]
    return jnp.where(slot_ids == longest[:, None], LMAX - 128, base).astype(jnp.int32)


def query_values(key):
    first_key = jax.random.fold_in(key, 0)
    shape = (N_REQ * ROWS, N_HEAD, QPK, HD)
    values = jnp.clip(jax.random.normal(first_key, shape, jnp.float32), -6.0, 6.0)
    return values.reshape(N_REQ * ROWS, N_HEAD, QPK * HD).astype(jnp.bfloat16)


def draw_first_query(key, part):
    key = jax.random.fold_in(key, 5)
    return query_values(key)


def draw_second_query(key, part):
    key = jax.random.fold_in(key, 7)
    return query_values(key)


def level_of(key, extent, shards, smallest, top_value):
    def one(dim, shards_of):
        heights = jax.random.uniform(jax.random.fold_in(jax.random.fold_in(key, 6), dim), (shards_of,), jnp.float32, smallest / len(shards), top_value / len(shards))
        return jnp.repeat(jnp.exp(heights), extent[dim] // shards_of).reshape((-1,) + (1,) * (len(extent) - dim - 1))

    gain = one(*shards[0])
    for cut in shards[1:]:
        gain = gain * one(*cut)
    return gain


def noise(key, extent, spread, reach, cuts=(), held_as=jnp.bfloat16):
    gain = level_of(key, extent, cuts, -0.22, 0.18) if cuts else 1.0
    values = jax.random.normal(key, extent, jnp.float32) * spread * gain
    return jnp.minimum(jnp.maximum(values, -reach), reach).astype(held_as)


def setup_inputs(seed: int = 0) -> dict:
    key_of = jax.random.split(jax.random.key(seed), 11)
    kv_cache = noise(key_of[0], (GROUPS * ROWS, KV_HEADS, LMAX, ENTRY), 1.0, 6.0, ((0, 64), (1, 4)))
    first_fresh = noise(key_of[1], (GROUPS * ROWS, KV_HEADS, ENTRY), 1.0, 6.0, ((0, 64), (1, 4)))
    second_fresh = noise(key_of[2], (GROUPS * ROWS, KV_HEADS, ENTRY), 1.0, 6.0, ((0, 64), (1, 4)))
    first_query = draw_first_query(jax.random.fold_in(key_of[10], 71), 0)
    second_query = draw_second_query(jax.random.fold_in(key_of[10], 71), 0)
    key_basis = noise(key_of[5], (KV_HEADS, RANK, HD), RANK ** -0.5, 0.75, ((0, 4),))
    out_weight = noise(key_of[6], (KV_HEADS * QPK * HD, D), 16 ** -0.5, 1.5, ((0, 4),))
    lengths = draw_lengths(jax.random.fold_in(key_of[10], 71), 0)
    leave_slot = draw_leave_slot(jax.random.fold_in(key_of[10], 71), 0)
    arrive_row = draw_arrive_row(jax.random.fold_in(key_of[10], 71), 0)
    return dict(kv_cache=kv_cache, first_fresh=first_fresh, second_fresh=second_fresh, first_query=first_query, second_query=second_query, key_basis=key_basis, out_weight=out_weight, lengths=lengths, leave_slot=leave_slot, arrive_row=arrive_row)


def insert_token(cache_rows, fresh_rows, position):
    slots = jnp.arange(cache_rows.shape[2], dtype=jnp.int32)
    hit_mask = slots[None, None, :, None] == position[:, None, None, None]
    return jnp.where(hit_mask, fresh_rows[:, :, None, :], cache_rows)

def attend_rows(cache_rows, position, query_rows, key_basis, out_weight):
    row_count = cache_rows.shape[0]
    factors = cache_rows[..., :RANK].astype(jnp.float32)
    value_part = cache_rows[..., RANK:].astype(jnp.float32)
    queries = query_rows.reshape(row_count, N_HEAD, QPK, HD).astype(jnp.float32)
    reduced = jnp.einsum('rhqe,hke->rhqk', queries, key_basis.astype(jnp.float32)).astype(jnp.bfloat16)
    scores = jnp.einsum('rhtk,rhqk->rhqt', factors, reduced.astype(jnp.float32)) * (1.0 / math.sqrt(HD))
    live_mask = jnp.arange(LMAX, dtype=jnp.int32)[None, None, None, :] <= position[:, None, None, None]
    scores = jnp.where(live_mask, scores, -1e+30)
    highest = lax.optimization_barrier(jnp.max(scores, axis=-1, keepdims=True))
    raw_weights = jnp.exp(scores - highest)
    weights = (raw_weights / lax.optimization_barrier(jnp.sum(raw_weights, axis=-1, keepdims=True))).astype(jnp.bfloat16)
    attended = jnp.einsum('rhqt,rhte->rhqe', weights.astype(jnp.float32), value_part).astype(jnp.bfloat16)
    attended = attended.reshape(row_count, N_HEAD * QPK * HD)
    return jnp.dot(attended, out_weight, preferred_element_type=jnp.float32).astype(jnp.bfloat16)

def run_step(cache_all, position, query_all, key_basis, out_weight):

    def one_group(pieces):
        return attend_rows(pieces[0], pieces[1], pieces[2], key_basis, out_weight)
    grouped = (cache_all.reshape(N_REQ, ROWS, N_HEAD, LMAX, RANK + HD), position.reshape(N_REQ, ROWS), query_all.reshape(N_REQ, ROWS, N_HEAD, QPK * HD))
    return lax.map(one_group, grouped).reshape(N_REQ * ROWS, D)

def reference(kv_cache, first_fresh, second_fresh, first_query, second_query, key_basis, out_weight, lengths, leave_slot, arrive_row):
    flat_len = lengths.reshape(-1).astype(jnp.int32)
    first_cache = insert_token(kv_cache, first_fresh, flat_len)
    first_out = run_step(first_cache, flat_len, first_query, key_basis, out_weight)
    sources = (jnp.arange(N_REQ, dtype=jnp.int32)[:, None] * ROWS + leave_slot).reshape(-1).astype(jnp.int32)
    targets = arrive_row.reshape(-1).astype(jnp.int32)
    moved_cache = first_cache.at[targets].set(first_cache[sources])
    moved_len = flat_len.at[targets].set(flat_len[sources])
    second_position = moved_len + 1
    final_cache = insert_token(moved_cache, second_fresh, second_position)
    second_out = run_step(final_cache, second_position, second_query, key_basis, out_weight)
    return (first_out, second_out, final_cache)
```

```python
import functools
import math

import jax
import jax.numpy as jnp
from jax import lax
from jax.experimental import pallas as pl
from jax.experimental.pallas import tpu as pltpu
from jax.sharding import PartitionSpec as P

MESH = pl.DeviceIdType.MESH
NT = (((1,), (1,)), ((), ()))
TILES = 48
BF16 = jnp.bfloat16
F32 = jnp.float32


def relay_place(index, head):
    pair = index // 6
    r = lax.rem(index, 6)
    y = pair // 2
    even = lax.rem(y + head, 2)
    main = r < 4
    x = 2 * lax.rem(pair, 2) + jnp.where(main, even, 1 - even)
    z_hi = jnp.where(main, r // 2, r - 4)
    core = jnp.where(main, lax.rem(r, 2), 0)
    return ((y * 2 + z_hi) * 4 + x) * 2 + core


def relay_role(me, head):
    core = lax.rem(me, 2)
    x = lax.rem(me // 2, 4)
    z_hi = lax.rem(me // 8, 2)
    y = me // 16
    pair = y * 2 + x // 2
    main = lax.rem(x, 2) == lax.rem(y + head, 2)
    index = pair * 6 + jnp.where(main, z_hi * 2 + core, 4 + z_hi)
    return jnp.logical_or(main, core == 0), index


def tile_of(q):
    return 16 * (q // 4), 128 * (q % 4)


def spread_columns(fresh):
    wide = fresh.astype(F32)
    rows = [jnp.broadcast_to(wide[s : s + 1], (128, 192)) for s in range(8)]
    rows = jnp.concatenate(rows, axis=0).astype(BF16)
    eye = (
        lax.broadcasted_iota(jnp.int32, (192, 192), 0)
        == lax.broadcasted_iota(jnp.int32, (192, 192), 1)
    ).astype(F32).astype(BF16)
    return lax.dot_general(eye, rows, NT, preferred_element_type=F32).astype(BF16)


def reduce_query(query, basis):
    wide = query.astype(F32)
    rows = jnp.concatenate([wide[:, 128 * q : 128 * q + 128] for q in range(8)], axis=0)
    tiled = jnp.concatenate([basis.astype(F32)] * 8, axis=0).astype(BF16)
    reduced = lax.dot_general(rows.astype(BF16), tiled, NT, preferred_element_type=F32)
    row = lax.broadcasted_iota(jnp.int32, (64, 512), 0)
    lane = lax.broadcasted_iota(jnp.int32, (64, 512), 1)
    return jnp.where(lax.rem(row, 8) == lane // 64, reduced, 0.0).astype(BF16)


def attend(cache, reduced, positions):
    factors = cache[:, 0:64, :].reshape(512, 512)
    scores = jnp.dot(reduced, factors, preferred_element_type=F32) * (1.0 / math.sqrt(128))
    slot = lax.rem(lax.broadcasted_iota(jnp.int32, (64, 512), 0), 8)
    token = lax.broadcasted_iota(jnp.int32, (64, 512), 1)
    limit = jnp.zeros((64, 512), jnp.int32)
    for s in range(8):
        limit = jnp.where(slot == s, positions[s], limit)
    scores = jnp.where(token <= limit, scores, -1e30)
    raw = jnp.exp(scores - jnp.max(scores, axis=-1, keepdims=True))
    weights = raw / jnp.sum(raw, axis=-1, keepdims=True)
    total = jnp.zeros((64, 128), F32)
    for s in range(8):
        own = jnp.where(slot == s, weights, 0.0).astype(BF16)
        total = total + lax.dot_general(
            own, cache[s, 64:192, :], NT, preferred_element_type=F32
        )
    return jnp.concatenate([total[8 * q : 8 * q + 8] for q in range(8)], axis=1).astype(BF16)


def project(attended, weight, share):
    def block(t, carry):
        start = pl.multiple_of(t * 1024, 1024)
        low = jnp.dot(attended, weight[:, pl.ds(start, 512)], preferred_element_type=F32)
        high = jnp.dot(attended, weight[:, pl.ds(start + 512, 512)], preferred_element_type=F32)
        share[t] = jnp.concatenate([low, high], axis=0).astype(BF16)
        return carry

    lax.fori_loop(0, 4, block, 0)


def kernel(
    leave, arrive, lens, leave_v, kv_hbm, ff, sf, q1, q2, basis, w_hbm,
    out1, out2, cache_hbm,
    kv, w, fin, s1, r1, s2, r2, tab_v, tab, cols, share1, share2, got1, got2,
    local_sem, send_sem, recv_sem, share_send, share_recv,
):
    me = lax.axis_index("req")
    head = lax.axis_index("head")
    across = lax.rem(head + 2, 4)
    is_relay, relay = relay_role(me, head)

    load_kv = pltpu.make_async_copy(kv_hbm, kv, local_sem.at[0])
    load_kv.start()
    load_w = pltpu.make_async_copy(w_hbm, w, local_sem.at[1])
    load_w.start()

    barrier = pltpu.get_barrier_semaphore()

    def greet(k, carry):
        pl.semaphore_signal(
            barrier, inc=1, device_id=(lax.rem(me + k, 64), across), device_id_type=MESH
        )
        return carry

    lax.fori_loop(0, 64, greet, 0)
    for d in (1, 3):
        pl.semaphore_signal(
            barrier, inc=1, device_id=(me, lax.rem(head + d, 4)), device_id_type=MESH
        )

    lane = lax.broadcasted_iota(jnp.int32, (16, 128), 1)
    p1 = [lens[s, me] for s in range(8)]
    cols[...] = spread_columns(ff[...])
    load_kv.wait()
    for s in range(8):
        for v in range(4):
            hit = lane + 128 * v == p1[s]
            for u in range(12):
                at = (s, pl.ds(16 * u, 16), pl.ds(128 * v, 128))
                fresh = cols[pl.ds(16 * u, 16), pl.ds(128 * s, 128)]
                kv[at] = jnp.where(hit, fresh.astype(F32), kv[at].astype(F32)).astype(BF16)
    for m in range(4):
        row = leave[m, me]
        for q in range(TILES):
            a, b = tile_of(q)
            s1[q, m] = kv[row, a : a + 16, b : b + 128]

    pl.semaphore_wait(barrier, 66)

    def spread(k, carry):
        q = lax.rem(k + me, TILES)
        pltpu.make_async_remote_copy(
            src_ref=s1.at[q], dst_ref=r1.at[me], send_sem=send_sem.at[0], recv_sem=recv_sem.at[0],
            device_id=(relay_place(q, head), across), device_id_type=MESH,
        ).start()
        return carry

    lax.fori_loop(0, TILES, spread, 0)

    place = 8 * lax.broadcasted_iota(jnp.int32, (4, 64), 1) + leave_v[...]

    def look(g, found):
        for m in range(4):
            found = jnp.where(place == arrive[m, g], 4 * g + m, found)
        return found

    tab_v[...] = lax.fori_loop(0, 64, look, jnp.zeros((4, 64), jnp.int32))
    copy_tab = pltpu.make_async_copy(tab_v, tab, local_sem.at[2])
    copy_tab.start()

    def share_out(share, got, which):
        for d in (1, 2, 3):
            to = lax.rem(head + d, 4)
            pltpu.make_async_remote_copy(
                src_ref=share.at[to], dst_ref=got.at[d - 1], send_sem=share_send.at[which],
                recv_sem=share_recv.at[which], device_id=(me, to), device_id_type=MESH,
            ).start()

    def share_in(share, got, which, out):
        pltpu.make_async_copy(got, got, share_recv.at[which]).wait()
        total = share[head].astype(F32)
        for d in range(3):
            total = total + got[d].astype(F32)
        out[...] = jnp.concatenate([total[0:8], total[8:16]], axis=1).astype(BF16)
        pltpu.make_async_copy(got, got, share_send.at[which]).wait()

    attended1 = attend(kv, reduce_query(q1[...], basis[...]), p1)
    load_w.wait()
    project(attended1, w, share1)
    share_out(share1, got1, 0)
    cols[...] = spread_columns(sf[...])
    reduced2 = reduce_query(q2[...], basis[...])

    copy_tab.wait()
    pltpu.make_async_copy(s1, s1, send_sem.at[0]).wait()

    @pl.when(is_relay)
    def _():
        pltpu.make_async_copy(r1, r1, recv_sem.at[0]).wait()

        def pick(j, carry):
            for a in range(4):
                s2[j, a] = r1[tab[a, j] // 4, lax.rem(tab[a, j], 4)]
            return carry

        lax.fori_loop(0, 64, pick, 0)

        def deliver(k, carry):
            j = lax.rem(k + me, 64)
            pltpu.make_async_remote_copy(
                src_ref=s2.at[j], dst_ref=r2.at[relay], send_sem=send_sem.at[1],
                recv_sem=recv_sem.at[1], device_id=(j, across), device_id_type=MESH,
            ).start()
            return carry

        lax.fori_loop(0, 64, deliver, 0)

    share_in(share1, got1, 0, out1)
    pltpu.make_async_copy(r2, r2, recv_sem.at[1]).wait()

    p2 = []
    stores = []
    for s in range(8):
        come = jnp.int32(0)
        stay = jnp.int32(1)
        for a in range(4):
            here = leave[a, me] == s
            come = jnp.where(here, a, come)
            stay = jnp.where(here, 0, stay)
        source = tab[come, me]
        group = source // 4
        length = jnp.where(stay == 1, p1[s], lens[leave[lax.rem(source, 4), group], group]) + 1
        p2.append(length)
        kept = jnp.full((16, 128), stay, jnp.int32) == 1
        for q in range(TILES):
            a, b = tile_of(q)
            tile = jnp.where(kept, kv[s, a : a + 16, b : b + 128].astype(F32), r2[q, come].astype(F32))
            fresh = cols[a : a + 16, 128 * s : 128 * s + 128].astype(F32)
            fin[s, a : a + 16, b : b + 128] = jnp.where(lane + b == length, fresh, tile).astype(BF16)
        store = pltpu.make_async_copy(fin.at[s], cache_hbm.at[s], local_sem.at[3 + s])
        store.start()
        stores.append(store)

    project(attend(fin, reduced2, p2), w, share2)
    share_out(share2, got2, 1)
    share_in(share2, got2, 1, out2)
    for store in stores:
        store.wait()

    @pl.when(is_relay)
    def _():
        pltpu.make_async_copy(s2, s2, send_sem.at[1]).wait()


def shards(
    kv_cache, first_fresh, second_fresh, first_query, second_query, key_basis, out_weight,
    lengths, leave_slot, arrive_row,
):
    kv = kv_cache[:, 0].transpose(0, 2, 1)
    smem = pl.BlockSpec(memory_space=pltpu.SMEM)
    vmem = pl.BlockSpec(memory_space=pltpu.VMEM)
    anywhere = pl.BlockSpec(memory_space=pl.ANY)
    out1, out2, cache = pl.pallas_call(
        kernel,
        out_shape=(
            jax.ShapeDtypeStruct((8, 1024), BF16),
            jax.ShapeDtypeStruct((8, 1024), BF16),
            jax.ShapeDtypeStruct((8, 192, 512), BF16),
        ),
        in_specs=[smem, smem, smem, vmem, anywhere] + [vmem] * 5 + [anywhere],
        out_specs=(vmem, vmem, anywhere),
        scratch_shapes=[
            pltpu.VMEM((8, 192, 512), BF16),
            pltpu.VMEM((1024, 4096), BF16),
            pltpu.VMEM((8, 192, 512), BF16),
            pltpu.VMEM((TILES, 4, 16, 128), BF16),
            pltpu.VMEM((64, 4, 16, 128), BF16),
            pltpu.VMEM((64, 4, 16, 128), BF16),
            pltpu.VMEM((TILES, 4, 16, 128), BF16),
            pltpu.VMEM((4, 64), jnp.int32),
            pltpu.SMEM((4, 64), jnp.int32),
            pltpu.VMEM((192, 1024), BF16),
            pltpu.VMEM((4, 16, 512), BF16),
            pltpu.VMEM((4, 16, 512), BF16),
            pltpu.VMEM((3, 16, 512), BF16),
            pltpu.VMEM((3, 16, 512), BF16),
            pltpu.SemaphoreType.DMA((11,)),
            pltpu.SemaphoreType.DMA((2,)),
            pltpu.SemaphoreType.DMA((2,)),
            pltpu.SemaphoreType.DMA((2,)),
            pltpu.SemaphoreType.DMA((2,)),
        ],
        compiler_params=pltpu.CompilerParams(
            collective_id=0, has_side_effects=True, vmem_limit_bytes=48 * 1024 * 1024
        ),
    )(
        leave_slot.T, arrive_row.T, lengths.T, leave_slot.T, kv,
        first_fresh[:, 0], second_fresh[:, 0], first_query[:, 0], second_query[:, 0],
        key_basis[0], out_weight,
    )
    return out1, out2, cache.transpose(0, 2, 1)[:, None]


def solution(mesh):
    placed = (
        P("req", "head", None, None),
        P("req", "head", None),
        P("req", "head", None),
        P("req", "head", None),
        P("req", "head", None),
        P("head", None, None),
        P("head", None),
        P(),
        P(),
        P(),
    )
    return jax.shard_map(
        shards,
        mesh=mesh,
        in_specs=placed,
        out_specs=(P("req", "head"), P("req", "head"), P("req", "head", None, None)),
        check_vma=False,
    )
```

```python
import functools
import math

import jax
import jax.numpy as jnp
from jax import lax
from jax.experimental import pallas as pl
from jax.experimental.pallas import tpu as pltpu
from jax.sharding import PartitionSpec as P

MESH = pl.DeviceIdType.MESH
NT = (((1,), (1,)), ((), ()))
TILES = 48
BF16 = jnp.bfloat16
F32 = jnp.float32


def hops(k):
    return (0, 1, 2, 1)[k // 16] + (0, 1, 2, 1)[k // 2 % 4]


FAR_FIRST = sorted(range(64), key=lambda k: (-hops(k), k))


def relay_place(index, head):
    pair = index // 6
    r = lax.rem(index, 6)
    y = pair // 2
    even = lax.rem(y + head, 2)
    main = r < 4
    x = 2 * lax.rem(pair, 2) + jnp.where(main, even, 1 - even)
    z_hi = jnp.where(main, r // 2, r - 4)
    core = jnp.where(main, lax.rem(r, 2), 0)
    return ((y * 2 + z_hi) * 4 + x) * 2 + core


def relay_role(me, head):
    core = lax.rem(me, 2)
    x = lax.rem(me // 2, 4)
    z_hi = lax.rem(me // 8, 2)
    y = me // 16
    pair = y * 2 + x // 2
    main = lax.rem(x, 2) == lax.rem(y + head, 2)
    index = pair * 6 + jnp.where(main, z_hi * 2 + core, 4 + z_hi)
    return jnp.logical_or(main, core == 0), index


def tile_of(q):
    return 16 * (q // 4), 128 * (q % 4)


def spread_columns(fresh):
    wide = fresh.astype(F32)
    rows = [jnp.broadcast_to(wide[s : s + 1], (128, 192)) for s in range(8)]
    rows = jnp.concatenate(rows, axis=0).astype(BF16)
    eye = (
        lax.broadcasted_iota(jnp.int32, (192, 192), 0)
        == lax.broadcasted_iota(jnp.int32, (192, 192), 1)
    ).astype(F32).astype(BF16)
    return lax.dot_general(eye, rows, NT, preferred_element_type=F32).astype(BF16)


def reduce_query(query, basis):
    wide = query.astype(F32)
    rows = jnp.concatenate([wide[:, 128 * q : 128 * q + 128] for q in range(8)], axis=0)
    tiled = jnp.concatenate([basis.astype(F32)] * 8, axis=0).astype(BF16)
    reduced = lax.dot_general(rows.astype(BF16), tiled, NT, preferred_element_type=F32)
    row = lax.broadcasted_iota(jnp.int32, (64, 512), 0)
    lane = lax.broadcasted_iota(jnp.int32, (64, 512), 1)
    return jnp.where(lax.rem(row, 8) == lane // 64, reduced, 0.0).astype(BF16)


def attend(cache, reduced, positions):
    factors = cache[:, 0:64, :].reshape(512, 512)
    scores = jnp.dot(reduced, factors, preferred_element_type=F32) * (1.0 / math.sqrt(128))
    slot = lax.rem(lax.broadcasted_iota(jnp.int32, (64, 512), 0), 8)
    token = lax.broadcasted_iota(jnp.int32, (64, 512), 1)
    limit = jnp.zeros((64, 512), jnp.int32)
    for s in range(8):
        limit = jnp.where(slot == s, positions[s], limit)
    scores = jnp.where(token <= limit, scores, -1e30)
    raw = jnp.exp(scores - jnp.max(scores, axis=-1, keepdims=True))
    weights = raw / jnp.sum(raw, axis=-1, keepdims=True)
    total = jnp.zeros((64, 128), F32)
    for s in range(8):
        own = jnp.where(slot == s, weights, 0.0).astype(BF16)
        total = total + lax.dot_general(
            own, cache[s, 64:192, :], NT, preferred_element_type=F32
        )
    return jnp.concatenate([total[8 * q : 8 * q + 8] for q in range(8)], axis=1).astype(BF16)


def project(attended, weight, share):
    def block(t, carry):
        start = pl.multiple_of(t * 1024, 1024)
        low = jnp.dot(attended, weight[:, pl.ds(start, 512)], preferred_element_type=F32)
        high = jnp.dot(attended, weight[:, pl.ds(start + 512, 512)], preferred_element_type=F32)
        share[t] = jnp.concatenate([low, high], axis=0).astype(BF16)
        return carry

    lax.fori_loop(0, 4, block, 0)


def kernel(
    leave_hbm, arrive_hbm, lens_hbm, kv_hbm, ff_hbm, sf_hbm, q1_hbm, q2_hbm, basis_hbm, w_hbm,
    out1_hbm, out2_hbm, cache_hbm,
    out1, out2, fin, leave, arrive, lens, leave_v, ff, sf, q1, q2, basis, kv, w, s1, r1, s2, r2, tab_v, tab, cols, share1, share2, got1, got2,
    local_sem, send_sem, recv_sem, share_send, share_recv,
):
    me = lax.axis_index("req")
    head = lax.axis_index("head")
    across = lax.rem(head + 2, 4)
    is_relay, relay = relay_role(me, head)

    loads = [
        pltpu.make_async_copy(source, target, local_sem.at[i])
        for i, (source, target) in enumerate(
            (
                (lens_hbm, lens),
                (leave_hbm, leave),
                (ff_hbm, ff),
                (kv_hbm, kv),
                (arrive_hbm, arrive),
                (leave_hbm, leave_v),
                (q1_hbm, q1),
                (basis_hbm, basis),
                (q2_hbm, q2),
                (sf_hbm, sf),
                (w_hbm, w),
            )
        )
    ]
    for load in loads:
        load.start()

    barrier = pltpu.get_barrier_semaphore()

    for k in FAR_FIRST:
        pl.semaphore_signal(
            barrier, inc=1, device_id=(jnp.bitwise_xor(me, k), across), device_id_type=MESH
        )
    for d in (1, 3):
        pl.semaphore_signal(
            barrier, inc=1, device_id=(me, lax.rem(head + d, 4)), device_id_type=MESH
        )

    lane = lax.broadcasted_iota(jnp.int32, (16, 128), 1)
    for load in loads[:3]:
        load.wait()
    p1 = [lens[s, me] for s in range(8)]
    cols[...] = spread_columns(ff[...])
    loads[3].wait()
    for s in range(8):
        for v in range(4):
            hit = lane + 128 * v == p1[s]
            for u in range(12):
                at = (s, pl.ds(16 * u, 16), pl.ds(128 * v, 128))
                fresh = cols[pl.ds(16 * u, 16), pl.ds(128 * s, 128)]
                kv[at] = jnp.where(hit, fresh.astype(F32), kv[at].astype(F32)).astype(BF16)
    for m in range(4):
        row = leave[m, me]
        for q in range(TILES):
            a, b = tile_of(q)
            s1[q, m] = kv[row, a : a + 16, b : b + 128]

    pl.semaphore_wait(barrier, 66)

    def spread(k, carry):
        q = lax.rem(k + me, TILES)
        pltpu.make_async_remote_copy(
            src_ref=s1.at[q], dst_ref=r1.at[me], send_sem=send_sem.at[0], recv_sem=recv_sem.at[0],
            device_id=(relay_place(q, head), across), device_id_type=MESH,
        ).start()
        return carry

    lax.fori_loop(0, TILES, spread, 0)

    for load in loads[4:10]:
        load.wait()

    place = 8 * lax.broadcasted_iota(jnp.int32, (4, 64), 1) + leave_v[...]

    def look(g, found):
        for m in range(4):
            found = jnp.where(place == arrive[m, g], 4 * g + m, found)
        return found

    tab_v[...] = lax.fori_loop(0, 64, look, jnp.zeros((4, 64), jnp.int32))
    copy_tab = pltpu.make_async_copy(tab_v, tab, local_sem.at[11])
    copy_tab.start()

    def share_out(share, got, which):
        for d in (1, 2, 3):
            to = lax.rem(head + d, 4)
            pltpu.make_async_remote_copy(
                src_ref=share.at[to], dst_ref=got.at[d - 1], send_sem=share_send.at[which],
                recv_sem=share_recv.at[which], device_id=(me, to), device_id_type=MESH,
            ).start()

    def share_in(share, got, which, out):
        pltpu.make_async_copy(got, got, share_recv.at[which]).wait()
        total = share[head].astype(F32)
        for d in range(3):
            total = total + got[d].astype(F32)
        out[...] = jnp.concatenate([total[0:8], total[8:16]], axis=1).astype(BF16)
        pltpu.make_async_copy(got, got, share_send.at[which]).wait()

    attended1 = attend(kv, reduce_query(q1[...], basis[...]), p1)
    loads[10].wait()
    project(attended1, w, share1)
    share_out(share1, got1, 0)
    cols[...] = spread_columns(sf[...])
    reduced2 = reduce_query(q2[...], basis[...])

    copy_tab.wait()
    pltpu.make_async_copy(s1, s1, send_sem.at[0]).wait()

    @pl.when(is_relay)
    def _():
        pltpu.make_async_copy(r1, r1, recv_sem.at[0]).wait()

        def pick(j, carry):
            for a in range(4):
                s2[j, a] = r1[tab[a, j] // 4, lax.rem(tab[a, j], 4)]
            return carry

        lax.fori_loop(0, 64, pick, 0)

        def deliver(k, carry):
            j = lax.rem(k + me, 64)
            pltpu.make_async_remote_copy(
                src_ref=s2.at[j], dst_ref=r2.at[relay], send_sem=send_sem.at[1],
                recv_sem=recv_sem.at[1], device_id=(j, across), device_id_type=MESH,
            ).start()
            return carry

        lax.fori_loop(0, 64, deliver, 0)

    share_in(share1, got1, 0, out1)
    pltpu.make_async_copy(r2, r2, recv_sem.at[1]).wait()

    p2 = []
    for s in range(8):
        come = jnp.int32(0)
        stay = jnp.int32(1)
        for a in range(4):
            here = leave[a, me] == s
            come = jnp.where(here, a, come)
            stay = jnp.where(here, 0, stay)
        source = tab[come, me]
        group = source // 4
        length = jnp.where(stay == 1, p1[s], lens[leave[lax.rem(source, 4), group], group]) + 1
        p2.append(length)
        kept = jnp.full((16, 128), stay, jnp.int32) == 1
        for q in range(TILES):
            a, b = tile_of(q)
            tile = jnp.where(kept, kv[s, a : a + 16, b : b + 128].astype(F32), r2[q, come].astype(F32))
            fresh = cols[a : a + 16, 128 * s : 128 * s + 128].astype(F32)
            fin[s, a : a + 16, b : b + 128] = jnp.where(lane + b == length, fresh, tile).astype(BF16)

    stores = [
        pltpu.make_async_copy(out1, out1_hbm, local_sem.at[12]),
        pltpu.make_async_copy(fin, cache_hbm, local_sem.at[13]),
    ]
    for store in stores:
        store.start()
    project(attend(fin, reduced2, p2), w, share2)
    share_out(share2, got2, 1)
    share_in(share2, got2, 1, out2)
    stores.append(pltpu.make_async_copy(out2, out2_hbm, local_sem.at[14]))
    stores[2].start()
    for store in stores:
        store.wait()

    @pl.when(is_relay)
    def _():
        pltpu.make_async_copy(s2, s2, send_sem.at[1]).wait()


def hand_over(out1, out2, cache, to1, to2, to_cache, held, held1, held2, sem_in, sem_out):
    ways = [(cache.at[s], held.at[s], to_cache.at[s]) for s in range(8)]
    ways += [(out1, held1, to1), (out2, held2, to2)]
    come = [pltpu.make_async_copy(a, b, sem_in.at[i]) for i, (a, b, c) in enumerate(ways)]
    go = [pltpu.make_async_copy(b, c, sem_out.at[i]) for i, (a, b, c) in enumerate(ways)]
    for copy in come:
        copy.start()
    for first, second in zip(come, go):
        first.wait()
        second.start()
    for copy in go:
        copy.wait()


def shards(
    kv_cache, first_fresh, second_fresh, first_query, second_query, key_basis, out_weight,
    lengths, leave_slot, arrive_row,
):
    kv = kv_cache[:, 0].transpose(0, 2, 1)
    hbm = pl.BlockSpec(memory_space=pltpu.HBM)
    out1, out2, cache = pl.pallas_call(
        kernel,
        out_shape=(
            jax.ShapeDtypeStruct((8, 1024), BF16),
            jax.ShapeDtypeStruct((8, 1024), BF16),
            jax.ShapeDtypeStruct((8, 192, 512), BF16),
        ),
        in_specs=[hbm] * 10,
        out_specs=(hbm, hbm, hbm),
        scratch_shapes=[
            pltpu.VMEM((8, 1024), BF16),
            pltpu.VMEM((8, 1024), BF16),
            pltpu.VMEM((8, 192, 512), BF16),
            pltpu.SMEM((4, 64), jnp.int32),
            pltpu.SMEM((4, 64), jnp.int32),
            pltpu.SMEM((8, 64), jnp.int32),
            pltpu.VMEM((4, 64), jnp.int32),
            pltpu.VMEM((8, 192), BF16),
            pltpu.VMEM((8, 192), BF16),
            pltpu.VMEM((8, 1024), BF16),
            pltpu.VMEM((8, 1024), BF16),
            pltpu.VMEM((64, 128), BF16),
            pltpu.VMEM((8, 192, 512), BF16),
            pltpu.VMEM((1024, 4096), BF16),
            pltpu.VMEM((TILES, 4, 16, 128), BF16),
            pltpu.VMEM((64, 4, 16, 128), BF16),
            pltpu.VMEM((64, 4, 16, 128), BF16),
            pltpu.VMEM((TILES, 4, 16, 128), BF16),
            pltpu.VMEM((4, 64), jnp.int32),
            pltpu.SMEM((4, 64), jnp.int32),
            pltpu.VMEM((192, 1024), BF16),
            pltpu.VMEM((4, 16, 512), BF16),
            pltpu.VMEM((4, 16, 512), BF16),
            pltpu.VMEM((3, 16, 512), BF16),
            pltpu.VMEM((3, 16, 512), BF16),
            pltpu.SemaphoreType.DMA((15,)),
            pltpu.SemaphoreType.DMA((2,)),
            pltpu.SemaphoreType.DMA((2,)),
            pltpu.SemaphoreType.DMA((2,)),
            pltpu.SemaphoreType.DMA((2,)),
        ],
        compiler_params=pltpu.CompilerParams(
            collective_id=0, has_side_effects=True, vmem_limit_bytes=60 * 1024 * 1024
        ),
    )(
        leave_slot.T, arrive_row.T, lengths.T, kv,
        first_fresh[:, 0], second_fresh[:, 0], first_query[:, 0], second_query[:, 0],
        key_basis[0], out_weight,
    )
    out1, out2, cache = pl.pallas_call(
        hand_over,
        out_shape=(
            jax.ShapeDtypeStruct((8, 1024), BF16),
            jax.ShapeDtypeStruct((8, 1024), BF16),
            jax.ShapeDtypeStruct((8, 192, 512), BF16),
        ),
        in_specs=[hbm] * 3,
        out_specs=(hbm, hbm, hbm),
        scratch_shapes=[pltpu.VMEM((8, 192, 512), BF16), pltpu.VMEM((8, 1024), BF16), pltpu.VMEM((8, 1024), BF16), pltpu.SemaphoreType.DMA((10,)), pltpu.SemaphoreType.DMA((10,))],
        compiler_params=pltpu.CompilerParams(vmem_limit_bytes=60 * 1024 * 1024),
    )(out1, out2, cache)
    return out1, out2, cache.transpose(0, 2, 1)[:, None]


def solution(mesh):
    placed = (
        P("req", "head", None, None),
        P("req", "head", None),
        P("req", "head", None),
        P("req", "head", None),
        P("req", "head", None),
        P("head", None, None),
        P("head", None),
        P(),
        P(),
        P(),
    )
    return jax.shard_map(
        shards,
        mesh=mesh,
        in_specs=placed,
        out_specs=(P("req", "head"), P("req", "head"), P("req", "head", None, None)),
        check_vma=False,
    )
```

```python
import functools
import math

import jax
import jax.numpy as jnp
from jax import lax
from jax.experimental import pallas as pl
from jax.experimental.pallas import tpu as pltpu
from jax.sharding import PartitionSpec as P

MESH = pl.DeviceIdType.MESH
NT = (((1,), (1,)), ((), ()))
TILES = 48
CROSS = 76
CROSS_PARTS = 2
BF16 = jnp.bfloat16
F32 = jnp.float32


def hops(k):
    return (0, 1, 2, 1)[k // 16] + (0, 1, 2, 1)[k // 2 % 4]


FAR_FIRST = sorted(range(64), key=lambda k: (-hops(k), k))
NEAR_FAR_FIRST = sorted(range(1, 32), key=lambda k: (-hops((k // 8) * 16 + k % 8), k))


def relay_place(index, head):
    pair = index // 6
    r = lax.rem(index, 6)
    y = pair // 2
    even = lax.rem(y + head, 2)
    main = r < 4
    x = 2 * lax.rem(pair, 2) + jnp.where(main, even, 1 - even)
    z_hi = jnp.where(main, r // 2, r - 4)
    core = jnp.where(main, lax.rem(r, 2), 0)
    return ((y * 2 + z_hi) * 4 + x) * 2 + core


def relay_role(me, head):
    core = lax.rem(me, 2)
    x = lax.rem(me // 2, 4)
    z_hi = lax.rem(me // 8, 2)
    y = me // 16
    pair = y * 2 + x // 2
    main = lax.rem(x, 2) == lax.rem(y + head, 2)
    index = pair * 6 + jnp.where(main, z_hi * 2 + core, 4 + z_hi)
    return jnp.logical_or(main, core == 0), index


def tile_of(q):
    return 16 * (q // 4), 128 * (q % 4)


def spread_columns(fresh):
    wide = fresh.astype(F32)
    rows = [jnp.broadcast_to(wide[s : s + 1], (128, 192)) for s in range(8)]
    rows = jnp.concatenate(rows, axis=0).astype(BF16)
    eye = (
        lax.broadcasted_iota(jnp.int32, (192, 192), 0)
        == lax.broadcasted_iota(jnp.int32, (192, 192), 1)
    ).astype(F32).astype(BF16)
    return lax.dot_general(eye, rows, NT, preferred_element_type=F32).astype(BF16)


def reduce_query(query, basis):
    wide = query.astype(F32)
    rows = jnp.concatenate([wide[:, 128 * q : 128 * q + 128] for q in range(8)], axis=0)
    tiled = jnp.concatenate([basis.astype(F32)] * 8, axis=0).astype(BF16)
    reduced = lax.dot_general(rows.astype(BF16), tiled, NT, preferred_element_type=F32)
    row = lax.broadcasted_iota(jnp.int32, (64, 512), 0)
    lane = lax.broadcasted_iota(jnp.int32, (64, 512), 1)
    return jnp.where(lax.rem(row, 8) == lane // 64, reduced, 0.0).astype(BF16)


def attend(cache, reduced, positions):
    factors = cache[:, 0:64, :].reshape(512, 512)
    scores = jnp.dot(reduced, factors, preferred_element_type=F32) * (1.0 / math.sqrt(128))
    slot = lax.rem(lax.broadcasted_iota(jnp.int32, (64, 512), 0), 8)
    token = lax.broadcasted_iota(jnp.int32, (64, 512), 1)
    limit = jnp.zeros((64, 512), jnp.int32)
    for s in range(8):
        limit = jnp.where(slot == s, positions[s], limit)
    scores = jnp.where(token <= limit, scores, -1e30)
    raw = jnp.exp(scores - jnp.max(scores, axis=-1, keepdims=True))
    weights = raw / jnp.sum(raw, axis=-1, keepdims=True)
    total = jnp.zeros((64, 128), F32)
    for s in range(8):
        own = jnp.where(slot == s, weights, 0.0).astype(BF16)
        total = total + lax.dot_general(
            own, cache[s, 64:192, :], NT, preferred_element_type=F32
        )
    return jnp.concatenate([total[8 * q : 8 * q + 8] for q in range(8)], axis=1).astype(BF16)


def project(attended, weight, share):
    def block(t, carry):
        start = pl.multiple_of(t * 1024, 1024)
        low = jnp.dot(attended, weight[:, pl.ds(start, 512)], preferred_element_type=F32)
        high = jnp.dot(attended, weight[:, pl.ds(start + 512, 512)], preferred_element_type=F32)
        share[t] = jnp.concatenate([low, high], axis=0).astype(BF16)
        return carry

    lax.fori_loop(0, 4, block, 0)


def general_kernel(
    leave_hbm, arrive_hbm, lens_hbm, kv_hbm, ff_hbm, sf_hbm, q1_hbm, q2_hbm, basis_hbm, w_hbm,
    out1_hbm, out2_hbm, cache_hbm,
    out1, out2, fin, leave, arrive, lens, leave_v, ff, sf, q1, q2, basis, kv, w, s1, r1, s2, r2, tab_v, tab, cols, share1, share2, got1, got2,
    local_sem, send_sem, recv_sem, share_send, share_recv,
):
    me = lax.axis_index("req")
    head = lax.axis_index("head")
    across = lax.rem(head + 2, 4)
    is_relay, relay = relay_role(me, head)

    loads = [
        pltpu.make_async_copy(source, target, local_sem.at[i])
        for i, (source, target) in enumerate(
            (
                (lens_hbm, lens),
                (leave_hbm, leave),
                (ff_hbm, ff),
                (kv_hbm, kv),
                (arrive_hbm, arrive),
                (leave_hbm, leave_v),
                (q1_hbm, q1),
                (basis_hbm, basis),
                (q2_hbm, q2),
                (sf_hbm, sf),
                (w_hbm, w),
            )
        )
    ]
    for load in loads:
        load.start()

    barrier = pltpu.get_barrier_semaphore()

    for k in FAR_FIRST:
        pl.semaphore_signal(
            barrier, inc=1, device_id=(jnp.bitwise_xor(me, k), across), device_id_type=MESH
        )
    for d in (1, 3):
        pl.semaphore_signal(
            barrier, inc=1, device_id=(me, lax.rem(head + d, 4)), device_id_type=MESH
        )

    lane = lax.broadcasted_iota(jnp.int32, (16, 128), 1)
    for load in loads[:3]:
        load.wait()
    p1 = [lens[s, me] for s in range(8)]
    cols[...] = spread_columns(ff[...])
    loads[3].wait()
    for s in range(8):
        for v in range(4):
            hit = lane + 128 * v == p1[s]
            for u in range(12):
                at = (s, pl.ds(16 * u, 16), pl.ds(128 * v, 128))
                fresh = cols[pl.ds(16 * u, 16), pl.ds(128 * s, 128)]
                kv[at] = jnp.where(hit, fresh.astype(F32), kv[at].astype(F32)).astype(BF16)
    for m in range(4):
        row = leave[m, me]
        for q in range(TILES):
            a, b = tile_of(q)
            s1[q, m] = kv[row, a : a + 16, b : b + 128]

    pl.semaphore_wait(barrier, 66)

    def spread(k, carry):
        q = lax.rem(k + me, TILES)
        pltpu.make_async_remote_copy(
            src_ref=s1.at[q], dst_ref=r1.at[me], send_sem=send_sem.at[0], recv_sem=recv_sem.at[0],
            device_id=(relay_place(q, head), across), device_id_type=MESH,
        ).start()
        return carry

    lax.fori_loop(0, TILES, spread, 0)

    for load in loads[4:10]:
        load.wait()

    place = 8 * lax.broadcasted_iota(jnp.int32, (4, 64), 1) + leave_v[...]

    def look(g, found):
        for m in range(4):
            found = jnp.where(place == arrive[m, g], 4 * g + m, found)
        return found

    tab_v[...] = lax.fori_loop(0, 64, look, jnp.zeros((4, 64), jnp.int32))
    copy_tab = pltpu.make_async_copy(tab_v, tab, local_sem.at[11])
    copy_tab.start()

    def share_out(share, got, which):
        for d in (1, 2, 3):
            to = lax.rem(head + d, 4)
            pltpu.make_async_remote_copy(
                src_ref=share.at[to], dst_ref=got.at[d - 1], send_sem=share_send.at[which],
                recv_sem=share_recv.at[which], device_id=(me, to), device_id_type=MESH,
            ).start()

    def share_in(share, got, which, out):
        pltpu.make_async_copy(got, got, share_recv.at[which]).wait()
        total = share[head].astype(F32)
        for d in range(3):
            total = total + got[d].astype(F32)
        out[...] = jnp.concatenate([total[0:8], total[8:16]], axis=1).astype(BF16)
        pltpu.make_async_copy(got, got, share_send.at[which]).wait()

    attended1 = attend(kv, reduce_query(q1[...], basis[...]), p1)
    loads[10].wait()
    project(attended1, w, share1)
    share_out(share1, got1, 0)
    cols[...] = spread_columns(sf[...])
    reduced2 = reduce_query(q2[...], basis[...])

    copy_tab.wait()
    pltpu.make_async_copy(s1, s1, send_sem.at[0]).wait()

    @pl.when(is_relay)
    def _():
        pltpu.make_async_copy(r1, r1, recv_sem.at[0]).wait()

        def pick(j, carry):
            for a in range(4):
                s2[j, a] = r1[tab[a, j] // 4, lax.rem(tab[a, j], 4)]
            return carry

        lax.fori_loop(0, 64, pick, 0)

        def deliver(k, carry):
            j = lax.rem(k + me, 64)
            pltpu.make_async_remote_copy(
                src_ref=s2.at[j], dst_ref=r2.at[relay], send_sem=send_sem.at[1],
                recv_sem=recv_sem.at[1], device_id=(j, across), device_id_type=MESH,
            ).start()
            return carry

        lax.fori_loop(0, 64, deliver, 0)

    share_in(share1, got1, 0, out1)
    pltpu.make_async_copy(r2, r2, recv_sem.at[1]).wait()

    p2 = []
    for s in range(8):
        come = jnp.int32(0)
        stay = jnp.int32(1)
        for a in range(4):
            here = leave[a, me] == s
            come = jnp.where(here, a, come)
            stay = jnp.where(here, 0, stay)
        source = tab[come, me]
        group = source // 4
        length = jnp.where(stay == 1, p1[s], lens[leave[lax.rem(source, 4), group], group]) + 1
        p2.append(length)
        kept = jnp.full((16, 128), stay, jnp.int32) == 1
        for q in range(TILES):
            a, b = tile_of(q)
            tile = jnp.where(kept, kv[s, a : a + 16, b : b + 128].astype(F32), r2[q, come].astype(F32))
            fresh = cols[a : a + 16, 128 * s : 128 * s + 128].astype(F32)
            fin[s, a : a + 16, b : b + 128] = jnp.where(lane + b == length, fresh, tile).astype(BF16)

    stores = [
        pltpu.make_async_copy(out1, out1_hbm, local_sem.at[12]),
        pltpu.make_async_copy(fin, cache_hbm, local_sem.at[13]),
    ]
    for store in stores:
        store.start()
    project(attend(fin, reduced2, p2), w, share2)
    share_out(share2, got2, 1)
    share_in(share2, got2, 1, out2)
    stores.append(pltpu.make_async_copy(out2, out2_hbm, local_sem.at[14]))
    stores[2].start()
    for store in stores:
        store.wait()

    @pl.when(is_relay)
    def _():
        pltpu.make_async_copy(s2, s2, send_sem.at[1]).wait()


def near_place(q, core, me, head):
    y = jnp.where(q == 12, 0, q // 3)
    k = jnp.where(q == 12, -1, lax.rem(q, 3))
    x = lax.rem(9 + core + k - y - head, 4)
    return y * 16 + lax.rem(me // 8, 2) * 8 + x * 2 + core


def group_at(plane, half):
    return (plane // 8) * 16 + half * 8 + lax.rem(plane, 8)


def fast_kernel(
    leave_hbm, arrive_hbm, lens_hbm, kv_hbm, ff_hbm, sf_hbm, q1_hbm, q2_hbm, basis_hbm, w_hbm,
    out1_hbm, out2_hbm, cache_hbm, fits,
    out1, out2, fin, leave, arrive, lens, leave_v, ff, sf, q1, q2, basis, kv, w,
    ft, s1, ra, rb, xs, both_a, both_b, s2, r2, r3, code_v, source_v, cross_v, code, source, cross,
    cols, cols1, share1, share2, got1, got2,
    local_sem, send_a, recv_a, send_b, recv_b, send_c, recv_c, share_send, share_recv,
):
    me = lax.axis_index("req")
    head = lax.axis_index("head")
    core = lax.rem(me, 2)
    x = lax.rem(me // 2, 4)
    half = lax.rem(me // 8, 2)
    y = me // 16
    plane = y * 8 + x * 2 + core
    turn = lax.rem(x + y + head + 3 * core, 4)
    is_fresh = jnp.logical_and(turn == 0, jnp.logical_and(y == 0, core == 0))
    is_relay1 = turn != 0
    is_relay0 = jnp.logical_or(is_relay1, is_fresh)
    my_q = jnp.where(turn == 0, 0, 3 * y + turn - 1)
    partner = jnp.bitwise_xor(me, 8)

    barrier = pltpu.get_barrier_semaphore()
    pl.semaphore_signal(barrier, inc=1, device_id=(partner, head), device_id_type=MESH)
    for k in NEAR_FAR_FIRST:
        to = jnp.bitwise_xor(me, (k // 8) * 16 + k % 8)
        pl.semaphore_signal(barrier, inc=1, device_id=(to, head), device_id_type=MESH)
    for d in (1, 2, 3):
        pl.semaphore_signal(
            barrier, inc=1, device_id=(me, lax.rem(head + d, 4)), device_id_type=MESH
        )

    loads = [
        pltpu.make_async_copy(origin, target, local_sem.at[i])
        for i, (origin, target) in enumerate(
            (
                (lens_hbm, lens),
                (leave_hbm, leave),
                (ff_hbm, ff),
                (kv_hbm, kv),
                (arrive_hbm, arrive),
                (leave_hbm, leave_v),
                (q1_hbm, q1),
                (basis_hbm, basis),
                (q2_hbm, q2),
                (sf_hbm, sf),
                (w_hbm, w),
            )
        )
    ]
    for load in loads:
        load.start()

    def post(src, dst, send, recv, to):
        @pl.when(to != me)
        def _():
            pltpu.make_async_remote_copy(
                src_ref=src, dst_ref=dst, send_sem=send, recv_sem=recv,
                device_id=(to, head), device_id_type=MESH,
            ).start()

        @pl.when(to == me)
        def _():
            pltpu.make_async_copy(src, dst, recv).start()

    def drain(ref, sem):
        pltpu.make_async_copy(ref, ref, sem).wait()

    lane = lax.broadcasted_iota(jnp.int32, (16, 128), 1)
    for load in loads[:3]:
        load.wait()
    p1 = [lens[s, me] for s in range(8)]
    cols[...] = spread_columns(ff[...])
    wide = ff[...].astype(F32)
    for s in range(8):
        low = wide[s : s + 1, 0:128]
        high = jnp.concatenate([wide[s : s + 1, 128:192], jnp.zeros((1, 64), F32)], axis=1)
        ft[s] = jnp.concatenate([low, high, jnp.zeros((14, 128), F32)], axis=0).astype(BF16)
    loads[3].wait()
    for s in range(8):
        for v in range(4):
            hit = lane + 128 * v == p1[s]
            for u in range(12):
                at = (s, pl.ds(16 * u, 16), pl.ds(128 * v, 128))
                fresh = cols[pl.ds(16 * u, 16), pl.ds(128 * s, 128)]
                kv[at] = jnp.where(hit, fresh.astype(F32), kv[at].astype(F32)).astype(BF16)

    rows = [leave[m, me] for m in range(4)]
    for m in range(4):
        s1[48, m] = ft[rows[m]]
    pl.semaphore_wait(barrier, 35)

    mine = pl.ds(4 * plane, 4)
    post(s1.at[48], ra.at[mine], send_a.at[0], recv_a.at[0], near_place(12, 0, me, head))
    def spread_tokens(v):
        landing = ra if v < 2 else rb

        def spread(k, carry):
            q = lax.rem(k + 3 * y + x, 12)
            for m in range(4):
                s1[12 * v + q, m] = kv[
                    rows[m], pl.ds(pl.multiple_of(16 * q, 16), 16), 128 * v : 128 * v + 128
                ]
            post(
                s1.at[12 * v + q], landing.at[mine], send_a.at[0], recv_a.at[v // 2],
                near_place(q, v % 2, me, head),
            )
            return carry

        lax.fori_loop(0, 12, spread, 0)

    spread_tokens(0)
    spread_tokens(1)
    for load in loads[4:10]:
        load.wait()

    place = 8 * lax.broadcasted_iota(jnp.int32, (4, 64), 1) + leave_v[...]
    lane_row = lax.broadcasted_iota(jnp.int32, (8, 128), 1)
    empty = jnp.zeros((4, 64), jnp.int32)
    carry = (empty, empty, jnp.full((8, 128), 0, jnp.int32))
    counts = []
    for side in range(2):

        def look(i, state, side=side):
            codes, sources, crosses, count = state
            group = group_at(i, side)
            for m in range(4):
                target = arrive[m, group]
                leaves = jnp.where(lax.rem(target // 64, 2) == side, 0, 1)
                index = 4 * i + m
                here = place == target
                codes = jnp.where(here, jnp.where(leaves == 1, 128 + count, index), codes)
                sources = jnp.where(here, 4 * group + m, sources)
                slot = jnp.where(jnp.logical_and(leaves == 1, half == side), count, -1)
                crosses = jnp.where(lane_row == slot, index, crosses)
                count = count + leaves
            return codes, sources, crosses, count

        *carry, count = lax.fori_loop(0, 32, look, (*carry, jnp.int32(0)))
        counts.append(count)
    code_v[...], source_v[...], cross_v[...] = carry
    code_v[...] = jnp.clip(code_v[...], 0, 127 + CROSS)
    tables = [
        pltpu.make_async_copy(code_v, code, local_sem.at[11]),
        pltpu.make_async_copy(source_v, source, local_sem.at[12]),
        pltpu.make_async_copy(cross_v, cross, local_sem.at[13]),
    ]
    stores = []
    fits[0, 0] = jnp.where(jnp.maximum(counts[0], counts[1]) <= CROSS, 1, 0)
    for copy in tables:
        copy.start()
    for copy in tables:
        copy.wait()

    def cross_over(i):
        held, landing = ((ra, both_a), (rb, both_b))[i]
        drain(held, recv_a.at[i])
        pltpu.make_async_copy(held, landing.at[pl.ds(0, 128)], recv_a.at[i]).start()
        part = CROSS // CROSS_PARTS

        for p in range(CROSS_PARTS):

            def pack(k, carry):
                xs[i, k] = held[cross[0, k]]
                return carry

            lax.fori_loop(p * part, p * part + part, pack, 0, unroll=2)
            pltpu.make_async_remote_copy(
                src_ref=xs.at[i, pl.ds(p * part, part)],
                dst_ref=landing.at[pl.ds(128 + p * part, part)],
                send_sem=send_b.at[i], recv_sem=recv_b.at[i],
                device_id=(partner, head), device_id_type=MESH,
            ).start()

    def deliver(i, target, sem):
        held, came = ((ra, both_a), (rb, both_b))[i]
        drain(held, recv_a.at[i])
        drain(xs.at[i], recv_b.at[i])

        def pick(j):
            group = group_at(j, half)
            for a in range(4):
                s2[i, j, a] = came[code[a, group]]

        def send(k, carry):
            j = jnp.bitwise_xor(plane, k)
            pick(j)
            pltpu.make_async_remote_copy(
                src_ref=s2.at[i, j], dst_ref=target, send_sem=send_c.at[i], recv_sem=sem,
                device_id=(group_at(j, half), head), device_id_type=MESH,
            ).start()
            return carry

        lax.fori_loop(1, 32, send, 0)
        pick(plane)
        pltpu.make_async_copy(s2.at[i, plane], target, sem).start()

    def share_out(attended, share, got, which):
        def block(d, carry):
            to = lax.rem(head + d, 4)
            start = pl.multiple_of(to * 1024, 1024)
            low = jnp.dot(attended, w[:, pl.ds(start, 512)], preferred_element_type=F32)
            high = jnp.dot(attended, w[:, pl.ds(start + 512, 512)], preferred_element_type=F32)
            share[to] = jnp.concatenate([low, high], axis=0).astype(BF16)

            @pl.when(d < 4)
            def _():
                pltpu.make_async_remote_copy(
                    src_ref=share.at[to], dst_ref=got.at[d - 1], send_sem=share_send.at[which],
                    recv_sem=share_recv.at[which], device_id=(me, to), device_id_type=MESH,
                ).start()

            return carry

        lax.fori_loop(1, 5, block, 0)

    def share_in(share, got, which, out):
        drain(got, share_recv.at[which])
        total = share[head].astype(F32)
        for d in range(3):
            total = total + got[d].astype(F32)
        out[...] = jnp.concatenate([total[0:8], total[8:16]], axis=1).astype(BF16)
        drain(got, share_send.at[which])

    @pl.when(is_relay0)
    def _():
        cross_over(0)

    spread_tokens(2)
    spread_tokens(3)
    attended1 = attend(kv, reduce_query(q1[...], basis[...]), p1)
    loads[10].wait()
    share_out(attended1, share1, got1, 0)

    @pl.when(jnp.logical_and(is_relay1, core == 0))
    def _():
        cross_over(1)

    cols[...] = spread_columns(sf[...])
    reduced2 = reduce_query(q2[...], basis[...])
    tile0 = jnp.where(is_fresh, 36, 12 * core + my_q)

    @pl.when(is_relay0)
    def _():
        deliver(0, r2.at[tile0], recv_c.at[0])

    @pl.when(jnp.logical_and(is_relay1, core == 1))
    def _():
        cross_over(1)

    share_in(share1, got1, 0, out1)
    stores.append(pltpu.make_async_copy(out1, out1_hbm, local_sem.at[15]))
    stores[-1].start()

    @pl.when(jnp.logical_and(is_relay1, core == 0))
    def _():
        deliver(1, r2.at[24 + my_q], recv_c.at[0])

    @pl.when(jnp.logical_and(is_relay1, core == 1))
    def _():
        deliver(1, r3.at[my_q], recv_c.at[1])

    comes, keeps, p2 = [], [], []
    drain(r2, recv_c.at[0])
    news = []
    lasts = []
    for s in range(8):
        come = jnp.int32(0)
        stay = jnp.int32(1)
        for a in range(4):
            here = leave[a, me] == s
            come = jnp.where(here, a, come)
            stay = jnp.where(here, 0, stay)
        origin = source[come, me]
        group = origin // 4
        last = jnp.where(stay == 1, p1[s], lens[leave[lax.rem(origin, 4), group], group])
        kept = jnp.full((16, 128), stay, jnp.int32) == 1
        comes.append(come)
        keeps.append(kept)
        lasts.append(last)
        p2.append(last + 1)
        new = jnp.where(kept, ft[s].astype(F32), r2[36, come].astype(F32))
        news.append(jnp.concatenate([new[0:1], new[1:2, 0:64]], axis=1))
    cols1[...] = spread_columns(jnp.concatenate(news, axis=0))

    def settle(s, u, v):
        a, b = 16 * u, 128 * v
        tile = jnp.where(
            keeps[s], kv[s, a : a + 16, b : b + 128].astype(F32), (r2[12 * v + u, comes[s]] if v < 3 else r3[u, comes[s]]).astype(F32)
        )
        fresh = cols[a : a + 16, 128 * s : 128 * s + 128].astype(F32)
        fin[s, a : a + 16, b : b + 128] = jnp.where(lane + b == p2[s], fresh, tile).astype(BF16)

    for s in range(8):
        for u in range(12):
            for v in range(3):
                settle(s, u, v)
            at = pl.ds(16 * u, 16)
            wide_s = pl.ds(128 * s, 128)
            tile = jnp.where(lane + 384 == lasts[s], cols1[at, wide_s].astype(F32), 0.0)
            tile = jnp.where(lane + 384 == p2[s], cols[at, wide_s].astype(F32), tile)
            fin[s, at, 384:512] = tile.astype(BF16)
    stores.append(
        pltpu.make_async_copy(
            fin.at[:, :, pl.ds(0, 384)], cache_hbm.at[:, :, pl.ds(0, 384)], local_sem.at[16]
        )
    )
    stores[-1].start()
    share_out(attend(fin, reduced2, p2), share2, got2, 1)

    drain(r3, recv_c.at[1])
    for s in range(8):
        for u in range(12):
            settle(s, u, 3)
    stores.append(
        pltpu.make_async_copy(
            fin.at[:, :, pl.ds(384, 128)], cache_hbm.at[:, :, pl.ds(384, 128)], local_sem.at[17]
        )
    )
    stores[-1].start()
    share_in(share2, got2, 1, out2)
    stores.append(pltpu.make_async_copy(out2, out2_hbm, local_sem.at[18]))
    stores[-1].start()

    drain(s1.at[pl.ds(0, 47)], send_a.at[0])

    @pl.when(turn == 0)
    def _():
        drain(s1.at[pl.ds(0, 1)], send_a.at[0])

    @pl.when(jnp.logical_and(turn == 0, jnp.logical_not(is_fresh)))
    def _():
        drain(s1.at[pl.ds(0, 1)], send_a.at[0])

    @pl.when(is_relay0)
    def _():
        drain(xs.at[0], send_b.at[0])
        drain(s2.at[0, pl.ds(0, 31)], send_c.at[0])

    @pl.when(is_relay1)
    def _():
        drain(xs.at[1], send_b.at[1])
        drain(s2.at[1, pl.ds(0, 31)], send_c.at[1])

    for store in stores:
        store.wait()


def hand_over(out1, out2, cache, to1, to2, to_cache, held, held1, held2, sem_in, sem_out):
    ways = [(cache.at[s], held.at[s], to_cache.at[s]) for s in range(8)]
    ways += [(out1, held1, to1), (out2, held2, to2)]
    come = [pltpu.make_async_copy(a, b, sem_in.at[i]) for i, (a, b, c) in enumerate(ways)]
    go = [pltpu.make_async_copy(b, c, sem_out.at[i]) for i, (a, b, c) in enumerate(ways)]
    for copy in come:
        copy.start()
    for first, second in zip(come, go):
        first.wait()
        second.start()
    for copy in go:
        copy.wait()


RESULTS = (
    jax.ShapeDtypeStruct((8, 1024), BF16),
    jax.ShapeDtypeStruct((8, 1024), BF16),
    jax.ShapeDtypeStruct((8, 192, 512), BF16),
)
COMMON = [
    pltpu.VMEM((8, 1024), BF16),
    pltpu.VMEM((8, 1024), BF16),
    pltpu.VMEM((8, 192, 512), BF16),
    pltpu.SMEM((4, 64), jnp.int32),
    pltpu.SMEM((4, 64), jnp.int32),
    pltpu.SMEM((8, 64), jnp.int32),
    pltpu.VMEM((4, 64), jnp.int32),
    pltpu.VMEM((8, 192), BF16),
    pltpu.VMEM((8, 192), BF16),
    pltpu.VMEM((8, 1024), BF16),
    pltpu.VMEM((8, 1024), BF16),
    pltpu.VMEM((64, 128), BF16),
    pltpu.VMEM((8, 192, 512), BF16),
    pltpu.VMEM((1024, 4096), BF16),
]
SHARES = [
    pltpu.VMEM((4, 16, 512), BF16),
    pltpu.VMEM((4, 16, 512), BF16),
    pltpu.VMEM((3, 16, 512), BF16),
    pltpu.VMEM((3, 16, 512), BF16),
]
PAIR = pltpu.SemaphoreType.DMA((2,))
HBM = pl.BlockSpec(memory_space=pltpu.HBM)


def run_general(*operands):
    return pl.pallas_call(
        general_kernel,
        out_shape=RESULTS,
        in_specs=[HBM] * 10,
        out_specs=[HBM] * 3,
        scratch_shapes=COMMON
        + [
            pltpu.VMEM((TILES, 4, 16, 128), BF16),
            pltpu.VMEM((64, 4, 16, 128), BF16),
            pltpu.VMEM((64, 4, 16, 128), BF16),
            pltpu.VMEM((TILES, 4, 16, 128), BF16),
            pltpu.VMEM((4, 64), jnp.int32),
            pltpu.SMEM((4, 64), jnp.int32),
            pltpu.VMEM((192, 1024), BF16),
        ]
        + SHARES
        + [pltpu.SemaphoreType.DMA((15,)), PAIR, PAIR, PAIR, PAIR],
        compiler_params=pltpu.CompilerParams(
            collective_id=1, has_side_effects=True, vmem_limit_bytes=60 * 1024 * 1024
        ),
    )(*operands)


def run_fast(*operands):
    return pl.pallas_call(
        fast_kernel,
        out_shape=RESULTS + (jax.ShapeDtypeStruct((1, 1), jnp.int32),),
        in_specs=[HBM] * 10,
        out_specs=[HBM] * 3 + [pl.BlockSpec(memory_space=pltpu.SMEM)],
        scratch_shapes=COMMON
        + [
            pltpu.VMEM((8, 16, 128), BF16),
            pltpu.VMEM((49, 4, 16, 128), BF16),
            pltpu.VMEM((128, 16, 128), BF16),
            pltpu.VMEM((128, 16, 128), BF16),
            pltpu.VMEM((2, CROSS, 16, 128), BF16),
            pltpu.VMEM((128 + CROSS, 16, 128), BF16),
            pltpu.VMEM((128 + CROSS, 16, 128), BF16),
            pltpu.VMEM((2, 32, 4, 16, 128), BF16),
            pltpu.VMEM((37, 4, 16, 128), BF16),
            pltpu.VMEM((12, 4, 16, 128), BF16),
            pltpu.VMEM((4, 64), jnp.int32),
            pltpu.VMEM((4, 64), jnp.int32),
            pltpu.VMEM((8, 128), jnp.int32),
            pltpu.SMEM((4, 64), jnp.int32),
            pltpu.SMEM((4, 64), jnp.int32),
            pltpu.SMEM((8, 128), jnp.int32),
            pltpu.VMEM((192, 1024), BF16),
            pltpu.VMEM((192, 1024), BF16),
        ]
        + SHARES
        + [pltpu.SemaphoreType.DMA((19,))]
        + [PAIR] * 8,
        compiler_params=pltpu.CompilerParams(
            collective_id=0, has_side_effects=True, vmem_limit_bytes=60 * 1024 * 1024
        ),
    )(*operands)


def pass_on(*results):
    return pl.pallas_call(
        hand_over,
        out_shape=RESULTS,
        in_specs=[HBM] * 3,
        out_specs=[HBM] * 3,
        scratch_shapes=[
            pltpu.VMEM((8, 192, 512), BF16),
            pltpu.VMEM((8, 1024), BF16),
            pltpu.VMEM((8, 1024), BF16),
            pltpu.SemaphoreType.DMA((10,)),
            pltpu.SemaphoreType.DMA((10,)),
        ],
        compiler_params=pltpu.CompilerParams(vmem_limit_bytes=60 * 1024 * 1024),
    )(*results)


def shards(
    kv_cache, first_fresh, second_fresh, first_query, second_query, key_basis, out_weight,
    lengths, leave_slot, arrive_row,
):
    operands = (
        leave_slot.T, arrive_row.T, lengths.T, kv_cache[:, 0].transpose(0, 2, 1),
        first_fresh[:, 0], second_fresh[:, 0], first_query[:, 0], second_query[:, 0],
        key_basis[0], out_weight,
    )
    *results, fits = run_fast(*operands)
    out1, out2, cache = lax.cond(
        fits[0, 0] == 1,
        lambda: tuple(pass_on(*results)),
        lambda: tuple(pass_on(*run_general(*operands))),
    )
    return out1, out2, cache.transpose(0, 2, 1)[:, None]


def solution(mesh):
    placed = (
        P("req", "head", None, None),
        P("req", "head", None),
        P("req", "head", None),
        P("req", "head", None),
        P("req", "head", None),
        P("head", None, None),
        P("head", None),
        P(),
        P(),
        P(),
    )
    return jax.shard_map(
        shards,
        mesh=mesh,
        in_specs=placed,
        out_specs=(P("req", "head"), P("req", "head"), P("req", "head", None, None)),
        check_vma=False,
    )
```

```python
import functools
import math

import jax
import jax.numpy as jnp
from jax import lax
from jax.experimental import pallas as pl
from jax.experimental.pallas import tpu as pltpu
from jax.sharding import PartitionSpec as P

MESH = pl.DeviceIdType.MESH
NT = (((1,), (1,)), ((), ()))
TILES = 48
CROSS = 76
CROSS_PARTS = 2
BF16 = jnp.bfloat16
F32 = jnp.float32


def hops(k):
    return (0, 1, 2, 1)[k // 16] + (0, 1, 2, 1)[k // 2 % 4]


FAR_FIRST = sorted(range(64), key=lambda k: (-hops(k), k))
NEAR_FAR_FIRST = sorted(range(1, 32), key=lambda k: (-hops((k // 8) * 16 + k % 8), k))


def relay_place(index, head):
    pair = index // 6
    r = lax.rem(index, 6)
    y = pair // 2
    even = lax.rem(y + head, 2)
    main = r < 4
    x = 2 * lax.rem(pair, 2) + jnp.where(main, even, 1 - even)
    z_hi = jnp.where(main, r // 2, r - 4)
    core = jnp.where(main, lax.rem(r, 2), 0)
    return ((y * 2 + z_hi) * 4 + x) * 2 + core


def relay_role(me, head):
    core = lax.rem(me, 2)
    x = lax.rem(me // 2, 4)
    z_hi = lax.rem(me // 8, 2)
    y = me // 16
    pair = y * 2 + x // 2
    main = lax.rem(x, 2) == lax.rem(y + head, 2)
    index = pair * 6 + jnp.where(main, z_hi * 2 + core, 4 + z_hi)
    return jnp.logical_or(main, core == 0), index


def tile_of(q):
    return 16 * (q // 4), 128 * (q % 4)


def spread_columns(fresh):
    wide = fresh.astype(F32)
    rows = [jnp.broadcast_to(wide[s : s + 1], (128, 192)) for s in range(8)]
    rows = jnp.concatenate(rows, axis=0).astype(BF16)
    eye = (
        lax.broadcasted_iota(jnp.int32, (192, 192), 0)
        == lax.broadcasted_iota(jnp.int32, (192, 192), 1)
    ).astype(F32).astype(BF16)
    return lax.dot_general(eye, rows, NT, preferred_element_type=F32).astype(BF16)


def reduce_query(query, basis):
    wide = query.astype(F32)
    rows = jnp.concatenate([wide[:, 128 * q : 128 * q + 128] for q in range(8)], axis=0)
    tiled = jnp.concatenate([basis.astype(F32)] * 8, axis=0).astype(BF16)
    reduced = lax.dot_general(rows.astype(BF16), tiled, NT, preferred_element_type=F32)
    row = lax.broadcasted_iota(jnp.int32, (64, 512), 0)
    lane = lax.broadcasted_iota(jnp.int32, (64, 512), 1)
    return jnp.where(lax.rem(row, 8) == lane // 64, reduced, 0.0).astype(BF16)


def attend(cache, reduced, positions):
    factors = cache[:, 0:64, :].reshape(512, 512)
    scores = jnp.dot(reduced, factors, preferred_element_type=F32) * (1.0 / math.sqrt(128))
    slot = lax.rem(lax.broadcasted_iota(jnp.int32, (64, 512), 0), 8)
    token = lax.broadcasted_iota(jnp.int32, (64, 512), 1)
    limit = jnp.zeros((64, 512), jnp.int32)
    for s in range(8):
        limit = jnp.where(slot == s, positions[s], limit)
    scores = jnp.where(token <= limit, scores, -1e30)
    raw = jnp.exp(scores - jnp.max(scores, axis=-1, keepdims=True))
    weights = raw / jnp.sum(raw, axis=-1, keepdims=True)
    total = jnp.zeros((64, 128), F32)
    for s in range(8):
        own = jnp.where(slot == s, weights, 0.0).astype(BF16)
        total = total + lax.dot_general(
            own, cache[s, 64:192, :], NT, preferred_element_type=F32
        )
    return jnp.concatenate([total[8 * q : 8 * q + 8] for q in range(8)], axis=1).astype(BF16)


def project(attended, weight, share):
    def block(t, carry):
        start = pl.multiple_of(t * 1024, 1024)
        low = jnp.dot(attended, weight[:, pl.ds(start, 512)], preferred_element_type=F32)
        high = jnp.dot(attended, weight[:, pl.ds(start + 512, 512)], preferred_element_type=F32)
        share[t] = jnp.concatenate([low, high], axis=0).astype(BF16)
        return carry

    lax.fori_loop(0, 4, block, 0)


def general_kernel(
    leave_hbm, arrive_hbm, lens_hbm, kv_hbm, ff_hbm, sf_hbm, q1_hbm, q2_hbm, basis_hbm, w_hbm,
    out1_hbm, out2_hbm, cache_hbm,
    out1, out2, fin, leave, arrive, lens, leave_v, ff, sf, q1, q2, basis, kv, w, s1, r1, s2, r2, tab_v, tab, cols, share1, share2, got1, got2,
    local_sem, send_sem, recv_sem, share_send, share_recv,
):
    me = lax.axis_index("req")
    head = lax.axis_index("head")
    across = lax.rem(head + 2, 4)
    is_relay, relay = relay_role(me, head)

    loads = [
        pltpu.make_async_copy(source, target, local_sem.at[i])
        for i, (source, target) in enumerate(
            (
                (lens_hbm, lens),
                (leave_hbm, leave),
                (ff_hbm, ff),
                (kv_hbm, kv),
                (arrive_hbm, arrive),
                (leave_hbm, leave_v),
                (q1_hbm, q1),
                (basis_hbm, basis),
                (q2_hbm, q2),
                (sf_hbm, sf),
                (w_hbm, w),
            )
        )
    ]
    for load in loads:
        load.start()

    barrier = pltpu.get_barrier_semaphore()

    for k in FAR_FIRST:
        pl.semaphore_signal(
            barrier, inc=1, device_id=(jnp.bitwise_xor(me, k), across), device_id_type=MESH
        )
    for d in (1, 3):
        pl.semaphore_signal(
            barrier, inc=1, device_id=(me, lax.rem(head + d, 4)), device_id_type=MESH
        )

    lane = lax.broadcasted_iota(jnp.int32, (16, 128), 1)
    for load in loads[:3]:
        load.wait()
    p1 = [lens[s, me] for s in range(8)]
    cols[...] = spread_columns(ff[...])
    loads[3].wait()
    for s in range(8):
        for v in range(4):
            hit = lane + 128 * v == p1[s]
            for u in range(12):
                at = (s, pl.ds(16 * u, 16), pl.ds(128 * v, 128))
                fresh = cols[pl.ds(16 * u, 16), pl.ds(128 * s, 128)]
                kv[at] = jnp.where(hit, fresh.astype(F32), kv[at].astype(F32)).astype(BF16)
    for m in range(4):
        row = leave[m, me]
        for q in range(TILES):
            a, b = tile_of(q)
            s1[q, m] = kv[row, a : a + 16, b : b + 128]

    pl.semaphore_wait(barrier, 66)

    def spread(k, carry):
        q = lax.rem(k + me, TILES)
        pltpu.make_async_remote_copy(
            src_ref=s1.at[q], dst_ref=r1.at[me], send_sem=send_sem.at[0], recv_sem=recv_sem.at[0],
            device_id=(relay_place(q, head), across), device_id_type=MESH,
        ).start()
        return carry

    lax.fori_loop(0, TILES, spread, 0)

    for load in loads[4:10]:
        load.wait()

    place = 8 * lax.broadcasted_iota(jnp.int32, (4, 64), 1) + leave_v[...]

    def look(g, found):
        for m in range(4):
            found = jnp.where(place == arrive[m, g], 4 * g + m, found)
        return found

    tab_v[...] = lax.fori_loop(0, 64, look, jnp.zeros((4, 64), jnp.int32))
    copy_tab = pltpu.make_async_copy(tab_v, tab, local_sem.at[11])
    copy_tab.start()

    def share_out(share, got, which):
        for d in (1, 2, 3):
            to = lax.rem(head + d, 4)
            pltpu.make_async_remote_copy(
                src_ref=share.at[to], dst_ref=got.at[d - 1], send_sem=share_send.at[which],
                recv_sem=share_recv.at[which], device_id=(me, to), device_id_type=MESH,
            ).start()

    def share_in(share, got, which, out):
        pltpu.make_async_copy(got, got, share_recv.at[which]).wait()
        total = share[head].astype(F32)
        for d in range(3):
            total = total + got[d].astype(F32)
        out[...] = jnp.concatenate([total[0:8], total[8:16]], axis=1).astype(BF16)
        pltpu.make_async_copy(got, got, share_send.at[which]).wait()

    attended1 = attend(kv, reduce_query(q1[...], basis[...]), p1)
    loads[10].wait()
    project(attended1, w, share1)
    share_out(share1, got1, 0)
    cols[...] = spread_columns(sf[...])
    reduced2 = reduce_query(q2[...], basis[...])

    copy_tab.wait()
    pltpu.make_async_copy(s1, s1, send_sem.at[0]).wait()

    @pl.when(is_relay)
    def _():
        pltpu.make_async_copy(r1, r1, recv_sem.at[0]).wait()

        def pick(j, carry):
            for a in range(4):
                s2[j, a] = r1[tab[a, j] // 4, lax.rem(tab[a, j], 4)]
            return carry

        lax.fori_loop(0, 64, pick, 0)

        def deliver(k, carry):
            j = lax.rem(k + me, 64)
            pltpu.make_async_remote_copy(
                src_ref=s2.at[j], dst_ref=r2.at[relay], send_sem=send_sem.at[1],
                recv_sem=recv_sem.at[1], device_id=(j, across), device_id_type=MESH,
            ).start()
            return carry

        lax.fori_loop(0, 64, deliver, 0)

    share_in(share1, got1, 0, out1)
    pltpu.make_async_copy(r2, r2, recv_sem.at[1]).wait()

    p2 = []
    for s in range(8):
        come = jnp.int32(0)
        stay = jnp.int32(1)
        for a in range(4):
            here = leave[a, me] == s
            come = jnp.where(here, a, come)
            stay = jnp.where(here, 0, stay)
        source = tab[come, me]
        group = source // 4
        length = jnp.where(stay == 1, p1[s], lens[leave[lax.rem(source, 4), group], group]) + 1
        p2.append(length)
        kept = jnp.full((16, 128), stay, jnp.int32) == 1
        for q in range(TILES):
            a, b = tile_of(q)
            tile = jnp.where(kept, kv[s, a : a + 16, b : b + 128].astype(F32), r2[q, come].astype(F32))
            fresh = cols[a : a + 16, 128 * s : 128 * s + 128].astype(F32)
            fin[s, a : a + 16, b : b + 128] = jnp.where(lane + b == length, fresh, tile).astype(BF16)

    stores = [
        pltpu.make_async_copy(out1, out1_hbm, local_sem.at[12]),
        pltpu.make_async_copy(fin, cache_hbm, local_sem.at[13]),
    ]
    for store in stores:
        store.start()
    project(attend(fin, reduced2, p2), w, share2)
    share_out(share2, got2, 1)
    share_in(share2, got2, 1, out2)
    stores.append(pltpu.make_async_copy(out2, out2_hbm, local_sem.at[14]))
    stores[2].start()
    for store in stores:
        store.wait()

    @pl.when(is_relay)
    def _():
        pltpu.make_async_copy(s2, s2, send_sem.at[1]).wait()


def near_place(q, core, me, head):
    y = jnp.where(q == 12, 0, q // 3)
    k = jnp.where(q == 12, -1, lax.rem(q, 3))
    x = lax.rem(9 + core + k - y - head, 4)
    return y * 16 + lax.rem(me // 8, 2) * 8 + x * 2 + core


def group_at(plane, half):
    return (plane // 8) * 16 + half * 8 + lax.rem(plane, 8)


def fast_kernel(
    leave_hbm, arrive_hbm, lens_hbm, kv_hbm, ff_hbm, sf_hbm, q1_hbm, q2_hbm, basis_hbm, w_hbm,
    out1_hbm, out2_hbm, cache_hbm, fits,
    out1, out2, fin, leave, arrive, lens, leave_v, ff, sf, q1, q2, basis, kv, w,
    ft, s1, ra, rb, xs, both_a, both_b, s2, r2, r3, code_v, source_v, cross_v, code, source, cross,
    cols, cols1, share1, share2, got1, got2,
    local_sem, send_a, recv_a, send_b, recv_b, send_c, recv_c, share_send, share_recv,
):
    me = lax.axis_index("req")
    head = lax.axis_index("head")
    core = lax.rem(me, 2)
    x = lax.rem(me // 2, 4)
    half = lax.rem(me // 8, 2)
    y = me // 16
    plane = y * 8 + x * 2 + core
    turn = lax.rem(x + y + head + 3 * core, 4)
    is_fresh = jnp.logical_and(turn == 0, jnp.logical_and(y == 0, core == 0))
    is_relay1 = turn != 0
    is_relay0 = jnp.logical_or(is_relay1, is_fresh)
    my_q = jnp.where(turn == 0, 0, 3 * y + turn - 1)
    partner = jnp.bitwise_xor(me, 8)

    barrier = pltpu.get_barrier_semaphore()
    pl.semaphore_signal(barrier, inc=1, device_id=(partner, head), device_id_type=MESH)
    for k in NEAR_FAR_FIRST:
        to = jnp.bitwise_xor(me, (k // 8) * 16 + k % 8)
        pl.semaphore_signal(barrier, inc=1, device_id=(to, head), device_id_type=MESH)
    for d in (1, 2, 3):
        pl.semaphore_signal(
            barrier, inc=1, device_id=(me, lax.rem(head + d, 4)), device_id_type=MESH
        )

    loads = [
        pltpu.make_async_copy(origin, target, local_sem.at[i])
        for i, (origin, target) in enumerate(
            (
                (lens_hbm, lens),
                (leave_hbm, leave),
                (ff_hbm, ff),
                (kv_hbm, kv),
                (arrive_hbm, arrive),
                (leave_hbm, leave_v),
                (q1_hbm, q1),
                (basis_hbm, basis),
                (q2_hbm, q2),
                (sf_hbm, sf),
                (w_hbm, w),
            )
        )
    ]
    for load in loads:
        load.start()

    def post(src, dst, send, recv, to):
        @pl.when(to != me)
        def _():
            pltpu.make_async_remote_copy(
                src_ref=src, dst_ref=dst, send_sem=send, recv_sem=recv,
                device_id=(to, head), device_id_type=MESH,
            ).start()

        @pl.when(to == me)
        def _():
            pltpu.make_async_copy(src, dst, recv).start()

    def drain(ref, sem):
        pltpu.make_async_copy(ref, ref, sem).wait()

    lane = lax.broadcasted_iota(jnp.int32, (16, 128), 1)
    for load in loads[:3]:
        load.wait()
    p1 = [lens[s, me] for s in range(8)]
    cols[...] = spread_columns(ff[...])
    wide = ff[...].astype(F32)
    for s in range(8):
        low = wide[s : s + 1, 0:128]
        high = jnp.concatenate([wide[s : s + 1, 128:192], jnp.zeros((1, 64), F32)], axis=1)
        ft[s] = jnp.concatenate([low, high, jnp.zeros((14, 128), F32)], axis=0).astype(BF16)
    loads[3].wait()
    for s in range(8):
        for v in range(4):
            hit = lane + 128 * v == p1[s]
            for u in range(12):
                at = (s, pl.ds(16 * u, 16), pl.ds(128 * v, 128))
                fresh = cols[pl.ds(16 * u, 16), pl.ds(128 * s, 128)]
                kv[at] = jnp.where(hit, fresh.astype(F32), kv[at].astype(F32)).astype(BF16)

    rows = [leave[m, me] for m in range(4)]
    for m in range(4):
        s1[48, m] = ft[rows[m]]
    pl.semaphore_wait(barrier, 35)

    mine = pl.ds(4 * plane, 4)
    post(s1.at[48], ra.at[mine], send_a.at[0], recv_a.at[0], near_place(12, 0, me, head))
    def spread_tokens(v):
        landing = ra if v < 2 else rb

        def spread(k, carry):
            q = lax.rem(k + 3 * y + x, 12)
            for m in range(4):
                s1[12 * v + q, m] = kv[
                    rows[m], pl.ds(pl.multiple_of(16 * q, 16), 16), 128 * v : 128 * v + 128
                ]
            post(
                s1.at[12 * v + q], landing.at[mine], send_a.at[0], recv_a.at[v // 2],
                near_place(q, v % 2, me, head),
            )
            return carry

        lax.fori_loop(0, 12, spread, 0)

    spread_tokens(0)
    spread_tokens(1)
    for load in loads[4:10]:
        load.wait()

    place = 8 * lax.broadcasted_iota(jnp.int32, (4, 64), 1) + leave_v[...]
    lane_row = lax.broadcasted_iota(jnp.int32, (8, 128), 1)
    empty = jnp.zeros((4, 64), jnp.int32)
    carry = (empty, empty, jnp.full((8, 128), 0, jnp.int32))
    counts = []
    for side in range(2):

        def look(i, state, side=side):
            codes, sources, crosses, count = state
            group = group_at(i, side)
            for m in range(4):
                target = arrive[m, group]
                leaves = jnp.where(lax.rem(target // 64, 2) == side, 0, 1)
                index = 4 * i + m
                here = place == target
                codes = jnp.where(here, jnp.where(leaves == 1, 128 + count, index), codes)
                sources = jnp.where(here, 4 * group + m, sources)
                slot = jnp.where(jnp.logical_and(leaves == 1, half == side), count, -1)
                crosses = jnp.where(lane_row == slot, index, crosses)
                count = count + leaves
            return codes, sources, crosses, count

        *carry, count = lax.fori_loop(0, 32, look, (*carry, jnp.int32(0)))
        counts.append(count)
    code_v[...], source_v[...], cross_v[...] = carry
    code_v[...] = jnp.clip(code_v[...], 0, 127 + CROSS)
    tables = [
        pltpu.make_async_copy(code_v, code, local_sem.at[11]),
        pltpu.make_async_copy(source_v, source, local_sem.at[12]),
        pltpu.make_async_copy(cross_v, cross, local_sem.at[13]),
    ]
    stores = []
    fits[0, 0] = jnp.where(jnp.maximum(counts[0], counts[1]) <= CROSS, 1, 0)
    for copy in tables:
        copy.start()
    for copy in tables:
        copy.wait()

    def cross_over(i):
        held, landing = ((ra, both_a), (rb, both_b))[i]
        drain(held, recv_a.at[i])
        pltpu.make_async_copy(held, landing.at[pl.ds(0, 128)], recv_a.at[i]).start()
        part = CROSS // CROSS_PARTS

        for p in range(CROSS_PARTS):

            def pack(k, carry):
                xs[i, k] = held[cross[0, k]]
                return carry

            lax.fori_loop(p * part, p * part + part, pack, 0, unroll=2)
            pltpu.make_async_remote_copy(
                src_ref=xs.at[i, pl.ds(p * part, part)],
                dst_ref=landing.at[pl.ds(128 + p * part, part)],
                send_sem=send_b.at[i], recv_sem=recv_b.at[i],
                device_id=(partner, head), device_id_type=MESH,
            ).start()

    def deliver(i, target, sem):
        held, came = ((ra, both_a), (rb, both_b))[i]
        drain(held, recv_a.at[i])
        drain(xs.at[i], recv_b.at[i])

        def pick(j):
            group = group_at(j, half)
            for a in range(4):
                s2[i, j, a] = came[code[a, group]]

        def send(k, carry):
            j = jnp.bitwise_xor(plane, k)
            pick(j)
            pltpu.make_async_remote_copy(
                src_ref=s2.at[i, j], dst_ref=target, send_sem=send_c.at[i], recv_sem=sem,
                device_id=(group_at(j, half), head), device_id_type=MESH,
            ).start()
            return carry

        lax.fori_loop(1, 32, send, 0)
        pick(plane)
        pltpu.make_async_copy(s2.at[i, plane], target, sem).start()

    def share_out(attended, share, got, which):
        def block(d, carry):
            to = lax.rem(head + d, 4)
            start = pl.multiple_of(to * 1024, 1024)
            low = jnp.dot(attended, w[:, pl.ds(start, 512)], preferred_element_type=F32)
            high = jnp.dot(attended, w[:, pl.ds(start + 512, 512)], preferred_element_type=F32)
            share[to] = jnp.concatenate([low, high], axis=0).astype(BF16)

            @pl.when(d < 4)
            def _():
                pltpu.make_async_remote_copy(
                    src_ref=share.at[to], dst_ref=got.at[d - 1], send_sem=share_send.at[which],
                    recv_sem=share_recv.at[which], device_id=(me, to), device_id_type=MESH,
                ).start()

            return carry

        lax.fori_loop(1, 5, block, 0)

    def share_in(share, got, which, out):
        drain(got, share_recv.at[which])
        total = share[head].astype(F32)
        for d in range(3):
            total = total + got[d].astype(F32)
        out[...] = jnp.concatenate([total[0:8], total[8:16]], axis=1).astype(BF16)
        drain(got, share_send.at[which])

    @pl.when(is_relay0)
    def _():
        cross_over(0)

    spread_tokens(2)
    spread_tokens(3)
    attended1 = attend(kv, reduce_query(q1[...], basis[...]), p1)
    loads[10].wait()
    share_out(attended1, share1, got1, 0)

    @pl.when(jnp.logical_and(is_relay1, core == 0))
    def _():
        cross_over(1)

    cols[...] = spread_columns(sf[...])
    reduced2 = reduce_query(q2[...], basis[...])
    tile0 = jnp.where(is_fresh, 36, 12 * core + my_q)

    @pl.when(is_relay0)
    def _():
        deliver(0, r2.at[tile0], recv_c.at[0])

    @pl.when(jnp.logical_and(is_relay1, core == 1))
    def _():
        cross_over(1)

    share_in(share1, got1, 0, out1)
    stores.append(pltpu.make_async_copy(out1, out1_hbm, local_sem.at[15]))
    stores[-1].start()

    @pl.when(jnp.logical_and(is_relay1, core == 0))
    def _():
        deliver(1, r2.at[24 + my_q], recv_c.at[0])

    @pl.when(jnp.logical_and(is_relay1, core == 1))
    def _():
        deliver(1, r3.at[my_q], recv_c.at[1])

    comes, keeps, p2 = [], [], []
    drain(r2, recv_c.at[0])
    news = []
    lasts = []
    for s in range(8):
        come = jnp.int32(0)
        stay = jnp.int32(1)
        for a in range(4):
            here = leave[a, me] == s
            come = jnp.where(here, a, come)
            stay = jnp.where(here, 0, stay)
        origin = source[come, me]
        group = origin // 4
        last = jnp.where(stay == 1, p1[s], lens[leave[lax.rem(origin, 4), group], group])
        kept = jnp.full((16, 128), stay, jnp.int32) == 1
        comes.append(come)
        keeps.append(kept)
        lasts.append(last)
        p2.append(last + 1)
        new = jnp.where(kept, ft[s].astype(F32), r2[36, come].astype(F32))
        news.append(jnp.concatenate([new[0:1], new[1:2, 0:64]], axis=1))
    cols1[...] = spread_columns(jnp.concatenate(news, axis=0))

    def settle(s, u, v):
        a, b = 16 * u, 128 * v
        tile = jnp.where(
            keeps[s], kv[s, a : a + 16, b : b + 128].astype(F32), (r2[12 * v + u, comes[s]] if v < 3 else r3[u, comes[s]]).astype(F32)
        )
        fresh = cols[a : a + 16, 128 * s : 128 * s + 128].astype(F32)
        fin[s, a : a + 16, b : b + 128] = jnp.where(lane + b == p2[s], fresh, tile).astype(BF16)

    for s in range(8):
        for u in range(12):
            for v in range(3):
                settle(s, u, v)
            at = pl.ds(16 * u, 16)
            wide_s = pl.ds(128 * s, 128)
            tile = jnp.where(lane + 384 == lasts[s], cols1[at, wide_s].astype(F32), 0.0)
            tile = jnp.where(lane + 384 == p2[s], cols[at, wide_s].astype(F32), tile)
            fin[s, at, 384:512] = tile.astype(BF16)
    stores.append(
        pltpu.make_async_copy(
            fin.at[:, :, pl.ds(0, 384)], cache_hbm.at[:, :, pl.ds(0, 384)], local_sem.at[16]
        )
    )
    stores[-1].start()
    share_out(attend(fin, reduced2, p2), share2, got2, 1)

    drain(r3, recv_c.at[1])
    for s in range(8):
        for u in range(12):
            settle(s, u, 3)
    stores.append(
        pltpu.make_async_copy(
            fin.at[:, :, pl.ds(384, 128)], cache_hbm.at[:, :, pl.ds(384, 128)], local_sem.at[17]
        )
    )
    stores[-1].start()
    share_in(share2, got2, 1, out2)
    stores.append(pltpu.make_async_copy(out2, out2_hbm, local_sem.at[18]))
    stores[-1].start()

    drain(s1.at[pl.ds(0, 47)], send_a.at[0])

    @pl.when(turn == 0)
    def _():
        drain(s1.at[pl.ds(0, 1)], send_a.at[0])

    @pl.when(jnp.logical_and(turn == 0, jnp.logical_not(is_fresh)))
    def _():
        drain(s1.at[pl.ds(0, 1)], send_a.at[0])

    @pl.when(is_relay0)
    def _():
        drain(xs.at[0], send_b.at[0])
        drain(s2.at[0, pl.ds(0, 31)], send_c.at[0])

    @pl.when(is_relay1)
    def _():
        drain(xs.at[1], send_b.at[1])
        drain(s2.at[1, pl.ds(0, 31)], send_c.at[1])

    for store in stores:
        store.wait()


def hand_over(out1, out2, cache, to1, to2, to_cache, held, held1, held2, sem_in, sem_out):
    ways = [(cache.at[s], held.at[s], to_cache.at[s]) for s in range(8)]
    ways += [(out1, held1, to1), (out2, held2, to2)]
    come = [pltpu.make_async_copy(a, b, sem_in.at[i]) for i, (a, b, c) in enumerate(ways)]
    go = [pltpu.make_async_copy(b, c, sem_out.at[i]) for i, (a, b, c) in enumerate(ways)]
    for copy in come:
        copy.start()
    for first, second in zip(come, go):
        first.wait()
        second.start()
    for copy in go:
        copy.wait()


RESULTS = (
    jax.ShapeDtypeStruct((8, 1024), BF16),
    jax.ShapeDtypeStruct((8, 1024), BF16),
    jax.ShapeDtypeStruct((8, 192, 512), BF16),
)
COMMON = [
    pltpu.VMEM((8, 1024), BF16),
    pltpu.VMEM((8, 1024), BF16),
    pltpu.VMEM((8, 192, 512), BF16),
    pltpu.SMEM((4, 64), jnp.int32),
    pltpu.SMEM((4, 64), jnp.int32),
    pltpu.SMEM((8, 64), jnp.int32),
    pltpu.VMEM((4, 64), jnp.int32),
    pltpu.VMEM((8, 192), BF16),
    pltpu.VMEM((8, 192), BF16),
    pltpu.VMEM((8, 1024), BF16),
    pltpu.VMEM((8, 1024), BF16),
    pltpu.VMEM((64, 128), BF16),
    pltpu.VMEM((8, 192, 512), BF16),
    pltpu.VMEM((1024, 4096), BF16),
]
SHARES = [
    pltpu.VMEM((4, 16, 512), BF16),
    pltpu.VMEM((4, 16, 512), BF16),
    pltpu.VMEM((3, 16, 512), BF16),
    pltpu.VMEM((3, 16, 512), BF16),
]
PAIR = pltpu.SemaphoreType.DMA((2,))
HBM = pl.BlockSpec(memory_space=pltpu.HBM)


def run_general(*operands):
    return pl.pallas_call(
        general_kernel,
        out_shape=RESULTS,
        in_specs=[HBM] * 10,
        out_specs=[HBM] * 3,
        scratch_shapes=COMMON
        + [
            pltpu.VMEM((TILES, 4, 16, 128), BF16),
            pltpu.VMEM((64, 4, 16, 128), BF16),
            pltpu.VMEM((64, 4, 16, 128), BF16),
            pltpu.VMEM((TILES, 4, 16, 128), BF16),
            pltpu.VMEM((4, 64), jnp.int32),
            pltpu.SMEM((4, 64), jnp.int32),
            pltpu.VMEM((192, 1024), BF16),
        ]
        + SHARES
        + [pltpu.SemaphoreType.DMA((15,)), PAIR, PAIR, PAIR, PAIR],
        compiler_params=pltpu.CompilerParams(
            collective_id=1, has_side_effects=True, vmem_limit_bytes=60 * 1024 * 1024
        ),
    )(*operands)


def run_fast(*operands):
    return pl.pallas_call(
        fast_kernel,
        out_shape=RESULTS + (jax.ShapeDtypeStruct((1, 1), jnp.int32),),
        in_specs=[HBM] * 10,
        out_specs=[HBM] * 3 + [pl.BlockSpec(memory_space=pltpu.SMEM)],
        scratch_shapes=COMMON
        + [
            pltpu.VMEM((8, 16, 128), BF16),
            pltpu.VMEM((49, 4, 16, 128), BF16),
            pltpu.VMEM((128, 16, 128), BF16),
            pltpu.VMEM((128, 16, 128), BF16),
            pltpu.VMEM((2, CROSS, 16, 128), BF16),
            pltpu.VMEM((128 + CROSS, 16, 128), BF16),
            pltpu.VMEM((128 + CROSS, 16, 128), BF16),
            pltpu.VMEM((2, 32, 4, 16, 128), BF16),
            pltpu.VMEM((37, 4, 16, 128), BF16),
            pltpu.VMEM((12, 4, 16, 128), BF16),
            pltpu.VMEM((4, 64), jnp.int32),
            pltpu.VMEM((4, 64), jnp.int32),
            pltpu.VMEM((8, 128), jnp.int32),
            pltpu.SMEM((4, 64), jnp.int32),
            pltpu.SMEM((4, 64), jnp.int32),
            pltpu.SMEM((8, 128), jnp.int32),
            pltpu.VMEM((192, 1024), BF16),
            pltpu.VMEM((192, 1024), BF16),
        ]
        + SHARES
        + [pltpu.SemaphoreType.DMA((19,))]
        + [PAIR] * 8,
        compiler_params=pltpu.CompilerParams(
            collective_id=0, has_side_effects=True, vmem_limit_bytes=60 * 1024 * 1024
        ),
    )(*operands)


def hand_straight(out1, out2, cache, to1, to2, to_cache, sem):
    copies = [
        pltpu.make_async_copy(cache.at[s], to_cache.at[s], sem.at[s]) for s in range(8)
    ]
    copies.append(pltpu.make_async_copy(out1, to1, sem.at[8]))
    copies.append(pltpu.make_async_copy(out2, to2, sem.at[9]))
    for copy in copies:
        copy.start()
    for copy in copies:
        copy.wait()


def pass_straight(*results):
    return pl.pallas_call(
        hand_straight,
        out_shape=RESULTS,
        in_specs=[pl.BlockSpec(memory_space=pltpu.VMEM)] * 3,
        out_specs=[HBM] * 3,
        scratch_shapes=[pltpu.SemaphoreType.DMA((10,))],
        compiler_params=pltpu.CompilerParams(vmem_limit_bytes=16 * 1024 * 1024),
    )(*results)


def pass_on(*results):
    return pl.pallas_call(
        hand_over,
        out_shape=RESULTS,
        in_specs=[HBM] * 3,
        out_specs=[HBM] * 3,
        scratch_shapes=[
            pltpu.VMEM((8, 192, 512), BF16),
            pltpu.VMEM((8, 1024), BF16),
            pltpu.VMEM((8, 1024), BF16),
            pltpu.SemaphoreType.DMA((10,)),
            pltpu.SemaphoreType.DMA((10,)),
        ],
        compiler_params=pltpu.CompilerParams(vmem_limit_bytes=60 * 1024 * 1024),
    )(*results)


def shards(
    kv_cache, first_fresh, second_fresh, first_query, second_query, key_basis, out_weight,
    lengths, leave_slot, arrive_row,
):
    operands = (
        leave_slot.T, arrive_row.T, lengths.T, kv_cache[:, 0].transpose(0, 2, 1),
        first_fresh[:, 0], second_fresh[:, 0], first_query[:, 0], second_query[:, 0],
        key_basis[0], out_weight,
    )
    *results, fits = run_fast(*operands)
    out1, out2, cache = lax.cond(
        fits[0, 0] == 1,
        lambda: tuple(pass_straight(*results)),
        lambda: tuple(pass_on(*run_general(*operands))),
    )
    return out1, out2, cache.transpose(0, 2, 1)[:, None]


def solution(mesh):
    placed = (
        P("req", "head", None, None),
        P("req", "head", None),
        P("req", "head", None),
        P("req", "head", None),
        P("req", "head", None),
        P("head", None, None),
        P("head", None),
        P(),
        P(),
        P(),
    )
    return jax.shard_map(
        shards,
        mesh=mesh,
        in_specs=placed,
        out_specs=(P("req", "head"), P("req", "head"), P("req", "head", None, None)),
        check_vma=False,
    )
```

```python
import functools
import math

import jax
import jax.numpy as jnp
from jax import lax
from jax.experimental import pallas as pl
from jax.experimental.pallas import tpu as pltpu
from jax.sharding import PartitionSpec as P

MESH = pl.DeviceIdType.MESH
NT = (((1,), (1,)), ((), ()))
TILES = 48
CROSS = 76
CROSS_PARTS = 2
BF16 = jnp.bfloat16
F32 = jnp.float32


def hops(k):
    return (0, 1, 2, 1)[k // 16] + (0, 1, 2, 1)[k // 2 % 4]


FAR_FIRST = sorted(range(64), key=lambda k: (-hops(k), k))
NEAR_FAR_FIRST = sorted(range(1, 32), key=lambda k: (-hops((k // 8) * 16 + k % 8), k))


def relay_place(index, head):
    pair = index // 6
    r = lax.rem(index, 6)
    y = pair // 2
    even = lax.rem(y + head, 2)
    main = r < 4
    x = 2 * lax.rem(pair, 2) + jnp.where(main, even, 1 - even)
    z_hi = jnp.where(main, r // 2, r - 4)
    core = jnp.where(main, lax.rem(r, 2), 0)
    return ((y * 2 + z_hi) * 4 + x) * 2 + core


def relay_role(me, head):
    core = lax.rem(me, 2)
    x = lax.rem(me // 2, 4)
    z_hi = lax.rem(me // 8, 2)
    y = me // 16
    pair = y * 2 + x // 2
    main = lax.rem(x, 2) == lax.rem(y + head, 2)
    index = pair * 6 + jnp.where(main, z_hi * 2 + core, 4 + z_hi)
    return jnp.logical_or(main, core == 0), index


def tile_of(q):
    return 16 * (q // 4), 128 * (q % 4)


def spread_columns(fresh):
    wide = fresh.astype(F32)
    rows = [jnp.broadcast_to(wide[s : s + 1], (128, 192)) for s in range(8)]
    rows = jnp.concatenate(rows, axis=0).astype(BF16)
    eye = (
        lax.broadcasted_iota(jnp.int32, (192, 192), 0)
        == lax.broadcasted_iota(jnp.int32, (192, 192), 1)
    ).astype(F32).astype(BF16)
    return lax.dot_general(eye, rows, NT, preferred_element_type=F32).astype(BF16)


def reduce_query(query, basis):
    wide = query.astype(F32)
    rows = jnp.concatenate([wide[:, 128 * q : 128 * q + 128] for q in range(8)], axis=0)
    tiled = jnp.concatenate([basis.astype(F32)] * 8, axis=0).astype(BF16)
    reduced = lax.dot_general(rows.astype(BF16), tiled, NT, preferred_element_type=F32)
    row = lax.broadcasted_iota(jnp.int32, (64, 512), 0)
    lane = lax.broadcasted_iota(jnp.int32, (64, 512), 1)
    return jnp.where(lax.rem(row, 8) == lane // 64, reduced, 0.0).astype(BF16)


def attend(cache, reduced, positions):
    factors = cache[:, 0:64, :].reshape(512, 512)
    scores = jnp.dot(reduced, factors, preferred_element_type=F32) * (1.0 / math.sqrt(128))
    slot = lax.rem(lax.broadcasted_iota(jnp.int32, (64, 512), 0), 8)
    token = lax.broadcasted_iota(jnp.int32, (64, 512), 1)
    limit = jnp.zeros((64, 512), jnp.int32)
    for s in range(8):
        limit = jnp.where(slot == s, positions[s], limit)
    scores = jnp.where(token <= limit, scores, -1e30)
    raw = jnp.exp(scores - jnp.max(scores, axis=-1, keepdims=True))
    weights = raw / jnp.sum(raw, axis=-1, keepdims=True)
    total = jnp.zeros((64, 128), F32)
    for s in range(8):
        own = jnp.where(slot == s, weights, 0.0).astype(BF16)
        total = total + lax.dot_general(
            own, cache[s, 64:192, :], NT, preferred_element_type=F32
        )
    return jnp.concatenate([total[8 * q : 8 * q + 8] for q in range(8)], axis=1).astype(BF16)


def project(attended, weight, share):
    def block(t, carry):
        start = pl.multiple_of(t * 1024, 1024)
        low = jnp.dot(attended, weight[:, pl.ds(start, 512)], preferred_element_type=F32)
        high = jnp.dot(attended, weight[:, pl.ds(start + 512, 512)], preferred_element_type=F32)
        share[t] = jnp.concatenate([low, high], axis=0).astype(BF16)
        return carry

    lax.fori_loop(0, 4, block, 0)


def general_kernel(
    leave_hbm, arrive_hbm, lens_hbm, kv_hbm, ff_hbm, sf_hbm, q1_hbm, q2_hbm, basis_hbm, w_hbm,
    out1_hbm, out2_hbm, cache_hbm,
    out1, out2, fin, leave, arrive, lens, leave_v, ff, sf, q1, q2, basis, kv, w, s1, r1, s2, r2, tab_v, tab, cols, share1, share2, got1, got2,
    local_sem, send_sem, recv_sem, share_send, share_recv,
):
    me = lax.axis_index("req")
    head = lax.axis_index("head")
    across = lax.rem(head + 2, 4)
    is_relay, relay = relay_role(me, head)

    loads = [
        pltpu.make_async_copy(source, target, local_sem.at[i])
        for i, (source, target) in enumerate(
            (
                (lens_hbm, lens),
                (leave_hbm, leave),
                (ff_hbm, ff),
                (kv_hbm, kv),
                (arrive_hbm, arrive),
                (leave_hbm, leave_v),
                (q1_hbm, q1),
                (basis_hbm, basis),
                (q2_hbm, q2),
                (sf_hbm, sf),
                (w_hbm, w),
            )
        )
    ]
    for load in loads:
        load.start()

    barrier = pltpu.get_barrier_semaphore()

    for k in FAR_FIRST:
        pl.semaphore_signal(
            barrier, inc=1, device_id=(jnp.bitwise_xor(me, k), across), device_id_type=MESH
        )
    for d in (1, 3):
        pl.semaphore_signal(
            barrier, inc=1, device_id=(me, lax.rem(head + d, 4)), device_id_type=MESH
        )

    lane = lax.broadcasted_iota(jnp.int32, (16, 128), 1)
    for load in loads[:3]:
        load.wait()
    p1 = [lens[s, me] for s in range(8)]
    cols[...] = spread_columns(ff[...])
    loads[3].wait()
    for s in range(8):
        for v in range(4):
            hit = lane + 128 * v == p1[s]
            for u in range(12):
                at = (s, pl.ds(16 * u, 16), pl.ds(128 * v, 128))
                fresh = cols[pl.ds(16 * u, 16), pl.ds(128 * s, 128)]
                kv[at] = jnp.where(hit, fresh.astype(F32), kv[at].astype(F32)).astype(BF16)
    for m in range(4):
        row = leave[m, me]
        for q in range(TILES):
            a, b = tile_of(q)
            s1[q, m] = kv[row, a : a + 16, b : b + 128]

    pl.semaphore_wait(barrier, 66)

    def spread(k, carry):
        q = lax.rem(k + me, TILES)
        pltpu.make_async_remote_copy(
            src_ref=s1.at[q], dst_ref=r1.at[me], send_sem=send_sem.at[0], recv_sem=recv_sem.at[0],
            device_id=(relay_place(q, head), across), device_id_type=MESH,
        ).start()
        return carry

    lax.fori_loop(0, TILES, spread, 0)

    for load in loads[4:10]:
        load.wait()

    place = 8 * lax.broadcasted_iota(jnp.int32, (4, 64), 1) + leave_v[...]

    def look(g, found):
        for m in range(4):
            found = jnp.where(place == arrive[m, g], 4 * g + m, found)
        return found

    tab_v[...] = lax.fori_loop(0, 64, look, jnp.zeros((4, 64), jnp.int32))
    copy_tab = pltpu.make_async_copy(tab_v, tab, local_sem.at[11])
    copy_tab.start()

    def share_out(share, got, which):
        for d in (1, 2, 3):
            to = lax.rem(head + d, 4)
            pltpu.make_async_remote_copy(
                src_ref=share.at[to], dst_ref=got.at[d - 1], send_sem=share_send.at[which],
                recv_sem=share_recv.at[which], device_id=(me, to), device_id_type=MESH,
            ).start()

    def share_in(share, got, which, out):
        pltpu.make_async_copy(got, got, share_recv.at[which]).wait()
        total = share[head].astype(F32)
        for d in range(3):
            total = total + got[d].astype(F32)
        out[...] = jnp.concatenate([total[0:8], total[8:16]], axis=1).astype(BF16)
        pltpu.make_async_copy(got, got, share_send.at[which]).wait()

    attended1 = attend(kv, reduce_query(q1[...], basis[...]), p1)
    loads[10].wait()
    project(attended1, w, share1)
    share_out(share1, got1, 0)
    cols[...] = spread_columns(sf[...])
    reduced2 = reduce_query(q2[...], basis[...])

    copy_tab.wait()
    pltpu.make_async_copy(s1, s1, send_sem.at[0]).wait()

    @pl.when(is_relay)
    def _():
        pltpu.make_async_copy(r1, r1, recv_sem.at[0]).wait()

        def pick(j, carry):
            for a in range(4):
                s2[j, a] = r1[tab[a, j] // 4, lax.rem(tab[a, j], 4)]
            return carry

        lax.fori_loop(0, 64, pick, 0)

        def deliver(k, carry):
            j = lax.rem(k + me, 64)
            pltpu.make_async_remote_copy(
                src_ref=s2.at[j], dst_ref=r2.at[relay], send_sem=send_sem.at[1],
                recv_sem=recv_sem.at[1], device_id=(j, across), device_id_type=MESH,
            ).start()
            return carry

        lax.fori_loop(0, 64, deliver, 0)

    share_in(share1, got1, 0, out1)
    pltpu.make_async_copy(r2, r2, recv_sem.at[1]).wait()

    p2 = []
    for s in range(8):
        come = jnp.int32(0)
        stay = jnp.int32(1)
        for a in range(4):
            here = leave[a, me] == s
            come = jnp.where(here, a, come)
            stay = jnp.where(here, 0, stay)
        source = tab[come, me]
        group = source // 4
        length = jnp.where(stay == 1, p1[s], lens[leave[lax.rem(source, 4), group], group]) + 1
        p2.append(length)
        kept = jnp.full((16, 128), stay, jnp.int32) == 1
        for q in range(TILES):
            a, b = tile_of(q)
            tile = jnp.where(kept, kv[s, a : a + 16, b : b + 128].astype(F32), r2[q, come].astype(F32))
            fresh = cols[a : a + 16, 128 * s : 128 * s + 128].astype(F32)
            fin[s, a : a + 16, b : b + 128] = jnp.where(lane + b == length, fresh, tile).astype(BF16)

    stores = [
        pltpu.make_async_copy(out1, out1_hbm, local_sem.at[12]),
        pltpu.make_async_copy(fin, cache_hbm, local_sem.at[13]),
    ]
    for store in stores:
        store.start()
    project(attend(fin, reduced2, p2), w, share2)
    share_out(share2, got2, 1)
    share_in(share2, got2, 1, out2)
    stores.append(pltpu.make_async_copy(out2, out2_hbm, local_sem.at[14]))
    stores[2].start()
    for store in stores:
        store.wait()

    @pl.when(is_relay)
    def _():
        pltpu.make_async_copy(s2, s2, send_sem.at[1]).wait()


def near_place(q, core, me, head):
    y = jnp.where(q == 12, 0, q // 3)
    k = jnp.where(q == 12, -1, lax.rem(q, 3))
    x = lax.rem(9 + core + k - y - head, 4)
    return y * 16 + lax.rem(me // 8, 2) * 8 + x * 2 + core


def group_at(plane, half):
    return (plane // 8) * 16 + half * 8 + lax.rem(plane, 8)


def fast_kernel(
    leave_hbm, arrive_hbm, lens_hbm, kv_hbm, ff_hbm, sf_hbm, q1_hbm, q2_hbm, basis_hbm, w_hbm,
    out1_hbm, out2_hbm, cache_hbm, fits,
    out1, out2, fin, leave, arrive, lens, leave_v, ff, sf, q1, q2, basis, kv, w,
    ft, s1, ra, rb, xs, both_a, both_b, s2, r2, r3, code_v, source_v, cross_v, code, source, cross,
    cols, cols1, share1, share2, got1, got2,
    local_sem, send_a, recv_a, send_b, recv_b, send_c, recv_c, share_send, share_recv,
):
    me = lax.axis_index("req")
    head = lax.axis_index("head")
    core = lax.rem(me, 2)
    x = lax.rem(me // 2, 4)
    half = lax.rem(me // 8, 2)
    y = me // 16
    plane = y * 8 + x * 2 + core
    turn = lax.rem(x + y + head + 3 * core, 4)
    is_fresh = jnp.logical_and(turn == 0, jnp.logical_and(y == 0, core == 0))
    is_relay1 = turn != 0
    is_relay0 = jnp.logical_or(is_relay1, is_fresh)
    my_q = jnp.where(turn == 0, 0, 3 * y + turn - 1)
    partner = jnp.bitwise_xor(me, 8)

    barrier = pltpu.get_barrier_semaphore()
    pl.semaphore_signal(barrier, inc=1, device_id=(partner, head), device_id_type=MESH)
    for k in NEAR_FAR_FIRST:
        to = jnp.bitwise_xor(me, (k // 8) * 16 + k % 8)
        pl.semaphore_signal(barrier, inc=1, device_id=(to, head), device_id_type=MESH)
    for d in (1, 2, 3):
        pl.semaphore_signal(
            barrier, inc=1, device_id=(me, lax.rem(head + d, 4)), device_id_type=MESH
        )

    loads = [
        pltpu.make_async_copy(origin, target, local_sem.at[i])
        for i, (origin, target) in enumerate(
            (
                (lens_hbm, lens),
                (leave_hbm, leave),
                (ff_hbm, ff),
                (kv_hbm, kv),
                (arrive_hbm, arrive),
                (leave_hbm, leave_v),
                (q1_hbm, q1),
                (basis_hbm, basis),
                (q2_hbm, q2),
                (sf_hbm, sf),
                (w_hbm, w),
            )
        )
    ]
    for load in loads:
        load.start()

    def post(src, dst, send, recv, to):
        @pl.when(to != me)
        def _():
            pltpu.make_async_remote_copy(
                src_ref=src, dst_ref=dst, send_sem=send, recv_sem=recv,
                device_id=(to, head), device_id_type=MESH,
            ).start()

        @pl.when(to == me)
        def _():
            pltpu.make_async_copy(src, dst, recv).start()

    def drain(ref, sem):
        pltpu.make_async_copy(ref, ref, sem).wait()

    lane = lax.broadcasted_iota(jnp.int32, (16, 128), 1)
    for load in loads[:3]:
        load.wait()
    p1 = [lens[s, me] for s in range(8)]
    cols[...] = spread_columns(ff[...])
    wide = ff[...].astype(F32)
    for s in range(8):
        low = wide[s : s + 1, 0:128]
        high = jnp.concatenate([wide[s : s + 1, 128:192], jnp.zeros((1, 64), F32)], axis=1)
        ft[s] = jnp.concatenate([low, high, jnp.zeros((14, 128), F32)], axis=0).astype(BF16)
    loads[3].wait()
    for s in range(8):
        for v in range(4):
            hit = lane + 128 * v == p1[s]
            for u in range(12):
                at = (s, pl.ds(16 * u, 16), pl.ds(128 * v, 128))
                fresh = cols[pl.ds(16 * u, 16), pl.ds(128 * s, 128)]
                kv[at] = jnp.where(hit, fresh, kv[at])

    rows = [leave[m, me] for m in range(4)]
    for m in range(4):
        s1[48, m] = ft[rows[m]]
    pl.semaphore_wait(barrier, 35)

    mine = pl.ds(4 * plane, 4)
    post(s1.at[48], ra.at[mine], send_a.at[0], recv_a.at[0], near_place(12, 0, me, head))
    def spread_tokens(v):
        landing = ra if v < 2 else rb

        def spread(k, carry):
            q = lax.rem(k + 3 * y + x, 12)
            for m in range(4):
                s1[12 * v + q, m] = kv[
                    rows[m], pl.ds(pl.multiple_of(16 * q, 16), 16), 128 * v : 128 * v + 128
                ]
            post(
                s1.at[12 * v + q], landing.at[mine], send_a.at[0], recv_a.at[v // 2],
                near_place(q, v % 2, me, head),
            )
            return carry

        lax.fori_loop(0, 12, spread, 0)

    spread_tokens(0)
    spread_tokens(1)
    spread_tokens(2)
    for load in loads[4:10]:
        load.wait()

    place = 8 * lax.broadcasted_iota(jnp.int32, (4, 64), 1) + leave_v[...]
    lane_row = lax.broadcasted_iota(jnp.int32, (8, 128), 1)
    empty = jnp.zeros((4, 64), jnp.int32)
    carry = (empty, empty, jnp.full((8, 128), 0, jnp.int32))
    counts = []
    for side in range(2):

        def look(i, state, side=side):
            codes, sources, crosses, count = state
            group = group_at(i, side)
            for m in range(4):
                target = arrive[m, group]
                leaves = jnp.where(lax.rem(target // 64, 2) == side, 0, 1)
                index = 4 * i + m
                here = place == target
                codes = jnp.where(here, jnp.where(leaves == 1, 128 + count, index), codes)
                sources = jnp.where(here, 4 * group + m, sources)
                slot = jnp.where(jnp.logical_and(leaves == 1, half == side), count, -1)
                crosses = jnp.where(lane_row == slot, index, crosses)
                count = count + leaves
            return codes, sources, crosses, count

        *carry, count = lax.fori_loop(0, 32, look, (*carry, jnp.int32(0)))
        counts.append(count)
    code_v[...], source_v[...], cross_v[...] = carry
    code_v[...] = jnp.clip(code_v[...], 0, 127 + CROSS)
    tables = [
        pltpu.make_async_copy(code_v, code, local_sem.at[11]),
        pltpu.make_async_copy(source_v, source, local_sem.at[12]),
        pltpu.make_async_copy(cross_v, cross, local_sem.at[13]),
    ]
    stores = []
    fits[0, 0] = jnp.where(jnp.maximum(counts[0], counts[1]) <= CROSS, 1, 0)
    for copy in tables:
        copy.start()
    for copy in tables:
        copy.wait()

    def cross_over(i):
        held, landing = ((ra, both_a), (rb, both_b))[i]
        drain(held, recv_a.at[i])
        pltpu.make_async_copy(held, landing.at[pl.ds(0, 128)], recv_a.at[i]).start()
        part = CROSS // CROSS_PARTS

        for p in range(CROSS_PARTS):

            def pack(k, carry):
                xs[i, k] = held[cross[0, k]]
                return carry

            lax.fori_loop(p * part, p * part + part, pack, 0, unroll=2)
            pltpu.make_async_remote_copy(
                src_ref=xs.at[i, pl.ds(p * part, part)],
                dst_ref=landing.at[pl.ds(128 + p * part, part)],
                send_sem=send_b.at[i], recv_sem=recv_b.at[i],
                device_id=(partner, head), device_id_type=MESH,
            ).start()

    def deliver(i, target, sem):
        held, came = ((ra, both_a), (rb, both_b))[i]
        drain(held, recv_a.at[i])
        drain(xs.at[i], recv_b.at[i])

        def pick(j):
            group = group_at(j, half)
            for a in range(4):
                s2[i, j, a] = came[code[a, group]]

        def send(k, carry):
            j = jnp.bitwise_xor(plane, k)
            pick(j)
            pltpu.make_async_remote_copy(
                src_ref=s2.at[i, j], dst_ref=target, send_sem=send_c.at[i], recv_sem=sem,
                device_id=(group_at(j, half), head), device_id_type=MESH,
            ).start()
            return carry

        lax.fori_loop(1, 32, send, 0)
        pick(plane)
        pltpu.make_async_copy(s2.at[i, plane], target, sem).start()

    def share_out(attended, share, got, which):
        def block(d, carry):
            to = lax.rem(head + d, 4)
            start = pl.multiple_of(to * 1024, 1024)
            low = jnp.dot(attended, w[:, pl.ds(start, 512)], preferred_element_type=F32)
            high = jnp.dot(attended, w[:, pl.ds(start + 512, 512)], preferred_element_type=F32)
            share[to] = jnp.concatenate([low, high], axis=0).astype(BF16)

            @pl.when(d < 4)
            def _():
                pltpu.make_async_remote_copy(
                    src_ref=share.at[to], dst_ref=got.at[d - 1], send_sem=share_send.at[which],
                    recv_sem=share_recv.at[which], device_id=(me, to), device_id_type=MESH,
                ).start()

            return carry

        lax.fori_loop(1, 5, block, 0)

    def share_in(share, got, which, out):
        drain(got, share_recv.at[which])
        total = share[head].astype(F32)
        for d in range(3):
            total = total + got[d].astype(F32)
        out[...] = jnp.concatenate([total[0:8], total[8:16]], axis=1).astype(BF16)
        drain(got, share_send.at[which])

    @pl.when(is_relay0)
    def _():
        cross_over(0)

    spread_tokens(3)
    attended1 = attend(kv, reduce_query(q1[...], basis[...]), p1)
    loads[10].wait()
    share_out(attended1, share1, got1, 0)

    @pl.when(jnp.logical_and(is_relay1, core == 0))
    def _():
        cross_over(1)

    cols[...] = spread_columns(sf[...])
    reduced2 = reduce_query(q2[...], basis[...])
    tile0 = jnp.where(is_fresh, 36, 12 * core + my_q)

    @pl.when(is_relay0)
    def _():
        deliver(0, r2.at[tile0], recv_c.at[0])

    @pl.when(jnp.logical_and(is_relay1, core == 1))
    def _():
        cross_over(1)

    share_in(share1, got1, 0, out1)
    stores.append(pltpu.make_async_copy(out1, out1_hbm, local_sem.at[15]))
    stores[-1].start()

    @pl.when(jnp.logical_and(is_relay1, core == 0))
    def _():
        deliver(1, r2.at[24 + my_q], recv_c.at[0])

    @pl.when(jnp.logical_and(is_relay1, core == 1))
    def _():
        deliver(1, r3.at[my_q], recv_c.at[1])

    comes, keeps, p2 = [], [], []
    drain(r2, recv_c.at[0])
    news = []
    lasts = []
    for s in range(8):
        come = jnp.int32(0)
        stay = jnp.int32(1)
        for a in range(4):
            here = leave[a, me] == s
            come = jnp.where(here, a, come)
            stay = jnp.where(here, 0, stay)
        origin = source[come, me]
        group = origin // 4
        last = jnp.where(stay == 1, p1[s], lens[leave[lax.rem(origin, 4), group], group])
        kept = jnp.full((16, 128), stay, jnp.int32) == 1
        comes.append(come)
        keeps.append(kept)
        lasts.append(last)
        p2.append(last + 1)
        new = jnp.where(kept, ft[s].astype(F32), r2[36, come].astype(F32))
        news.append(jnp.concatenate([new[0:1], new[1:2, 0:64]], axis=1))
    cols1[...] = spread_columns(jnp.concatenate(news, axis=0))

    def settle(s, u, v):
        a, b = 16 * u, 128 * v
        came = r2[12 * v + u, comes[s]] if v < 3 else r3[u, comes[s]]
        tile = jnp.where(keeps[s], kv[s, a : a + 16, b : b + 128], came)
        fresh = cols[a : a + 16, 128 * s : 128 * s + 128]
        fin[s, a : a + 16, b : b + 128] = jnp.where(lane + b == p2[s], fresh, tile)

    for s in range(8):
        for u in range(12):
            for v in range(3):
                settle(s, u, v)
            at = pl.ds(16 * u, 16)
            wide_s = pl.ds(128 * s, 128)
            tile = jnp.where(lane + 384 == lasts[s], cols1[at, wide_s].astype(F32), 0.0)
            tile = jnp.where(lane + 384 == p2[s], cols[at, wide_s].astype(F32), tile)
            fin[s, at, 384:512] = tile.astype(BF16)
    stores.append(
        pltpu.make_async_copy(
            fin.at[:, :, pl.ds(0, 384)], cache_hbm.at[:, :, pl.ds(0, 384)], local_sem.at[16]
        )
    )
    stores[-1].start()
    share_out(attend(fin, reduced2, p2), share2, got2, 1)

    drain(r3, recv_c.at[1])
    for s in range(8):
        for u in range(12):
            settle(s, u, 3)
    stores.append(
        pltpu.make_async_copy(
            fin.at[:, :, pl.ds(384, 128)], cache_hbm.at[:, :, pl.ds(384, 128)], local_sem.at[17]
        )
    )
    stores[-1].start()
    share_in(share2, got2, 1, out2)
    stores.append(pltpu.make_async_copy(out2, out2_hbm, local_sem.at[18]))
    stores[-1].start()

    drain(s1.at[pl.ds(0, 47)], send_a.at[0])

    @pl.when(turn == 0)
    def _():
        drain(s1.at[pl.ds(0, 1)], send_a.at[0])

    @pl.when(jnp.logical_and(turn == 0, jnp.logical_not(is_fresh)))
    def _():
        drain(s1.at[pl.ds(0, 1)], send_a.at[0])

    @pl.when(is_relay0)
    def _():
        drain(xs.at[0], send_b.at[0])
        drain(s2.at[0, pl.ds(0, 31)], send_c.at[0])

    @pl.when(is_relay1)
    def _():
        drain(xs.at[1], send_b.at[1])
        drain(s2.at[1, pl.ds(0, 31)], send_c.at[1])

    for store in stores:
        store.wait()


def hand_over(out1, out2, cache, to1, to2, to_cache, held, held1, held2, sem_in, sem_out):
    ways = [(cache.at[s], held.at[s], to_cache.at[s]) for s in range(8)]
    ways += [(out1, held1, to1), (out2, held2, to2)]
    come = [pltpu.make_async_copy(a, b, sem_in.at[i]) for i, (a, b, c) in enumerate(ways)]
    go = [pltpu.make_async_copy(b, c, sem_out.at[i]) for i, (a, b, c) in enumerate(ways)]
    for copy in come:
        copy.start()
    for first, second in zip(come, go):
        first.wait()
        second.start()
    for copy in go:
        copy.wait()


RESULTS = (
    jax.ShapeDtypeStruct((8, 1024), BF16),
    jax.ShapeDtypeStruct((8, 1024), BF16),
    jax.ShapeDtypeStruct((8, 192, 512), BF16),
)
COMMON = [
    pltpu.VMEM((8, 1024), BF16),
    pltpu.VMEM((8, 1024), BF16),
    pltpu.VMEM((8, 192, 512), BF16),
    pltpu.SMEM((4, 64), jnp.int32),
    pltpu.SMEM((4, 64), jnp.int32),
    pltpu.SMEM((8, 64), jnp.int32),
    pltpu.VMEM((4, 64), jnp.int32),
    pltpu.VMEM((8, 192), BF16),
    pltpu.VMEM((8, 192), BF16),
    pltpu.VMEM((8, 1024), BF16),
    pltpu.VMEM((8, 1024), BF16),
    pltpu.VMEM((64, 128), BF16),
    pltpu.VMEM((8, 192, 512), BF16),
    pltpu.VMEM((1024, 4096), BF16),
]
SHARES = [
    pltpu.VMEM((4, 16, 512), BF16),
    pltpu.VMEM((4, 16, 512), BF16),
    pltpu.VMEM((3, 16, 512), BF16),
    pltpu.VMEM((3, 16, 512), BF16),
]
PAIR = pltpu.SemaphoreType.DMA((2,))
HBM = pl.BlockSpec(memory_space=pltpu.HBM)


def run_general(*operands):
    return pl.pallas_call(
        general_kernel,
        out_shape=RESULTS,
        in_specs=[HBM] * 10,
        out_specs=[HBM] * 3,
        scratch_shapes=COMMON
        + [
            pltpu.VMEM((TILES, 4, 16, 128), BF16),
            pltpu.VMEM((64, 4, 16, 128), BF16),
            pltpu.VMEM((64, 4, 16, 128), BF16),
            pltpu.VMEM((TILES, 4, 16, 128), BF16),
            pltpu.VMEM((4, 64), jnp.int32),
            pltpu.SMEM((4, 64), jnp.int32),
            pltpu.VMEM((192, 1024), BF16),
        ]
        + SHARES
        + [pltpu.SemaphoreType.DMA((15,)), PAIR, PAIR, PAIR, PAIR],
        compiler_params=pltpu.CompilerParams(
            collective_id=1, has_side_effects=True, vmem_limit_bytes=60 * 1024 * 1024
        ),
    )(*operands)


def run_fast(*operands):
    return pl.pallas_call(
        fast_kernel,
        out_shape=RESULTS + (jax.ShapeDtypeStruct((1, 1), jnp.int32),),
        in_specs=[HBM] * 10,
        out_specs=[HBM] * 3 + [pl.BlockSpec(memory_space=pltpu.SMEM)],
        scratch_shapes=COMMON
        + [
            pltpu.VMEM((8, 16, 128), BF16),
            pltpu.VMEM((49, 4, 16, 128), BF16),
            pltpu.VMEM((128, 16, 128), BF16),
            pltpu.VMEM((128, 16, 128), BF16),
            pltpu.VMEM((2, CROSS, 16, 128), BF16),
            pltpu.VMEM((128 + CROSS, 16, 128), BF16),
            pltpu.VMEM((128 + CROSS, 16, 128), BF16),
            pltpu.VMEM((2, 32, 4, 16, 128), BF16),
            pltpu.VMEM((37, 4, 16, 128), BF16),
            pltpu.VMEM((12, 4, 16, 128), BF16),
            pltpu.VMEM((4, 64), jnp.int32),
            pltpu.VMEM((4, 64), jnp.int32),
            pltpu.VMEM((8, 128), jnp.int32),
            pltpu.SMEM((4, 64), jnp.int32),
            pltpu.SMEM((4, 64), jnp.int32),
            pltpu.SMEM((8, 128), jnp.int32),
            pltpu.VMEM((192, 1024), BF16),
            pltpu.VMEM((192, 1024), BF16),
        ]
        + SHARES
        + [pltpu.SemaphoreType.DMA((19,))]
        + [PAIR] * 8,
        compiler_params=pltpu.CompilerParams(
            collective_id=0, has_side_effects=True, vmem_limit_bytes=60 * 1024 * 1024
        ),
    )(*operands)


def hand_straight(out1, out2, cache, to1, to2, to_cache, sem):
    copies = [
        pltpu.make_async_copy(cache.at[s], to_cache.at[s], sem.at[s]) for s in range(8)
    ]
    copies.append(pltpu.make_async_copy(out1, to1, sem.at[8]))
    copies.append(pltpu.make_async_copy(out2, to2, sem.at[9]))
    for copy in copies:
        copy.start()
    for copy in copies:
        copy.wait()


def pass_straight(*results):
    return pl.pallas_call(
        hand_straight,
        out_shape=RESULTS,
        in_specs=[pl.BlockSpec(memory_space=pltpu.VMEM)] * 3,
        out_specs=[HBM] * 3,
        scratch_shapes=[pltpu.SemaphoreType.DMA((10,))],
        compiler_params=pltpu.CompilerParams(vmem_limit_bytes=16 * 1024 * 1024),
    )(*results)


def pass_on(*results):
    return pl.pallas_call(
        hand_over,
        out_shape=RESULTS,
        in_specs=[HBM] * 3,
        out_specs=[HBM] * 3,
        scratch_shapes=[
            pltpu.VMEM((8, 192, 512), BF16),
            pltpu.VMEM((8, 1024), BF16),
            pltpu.VMEM((8, 1024), BF16),
            pltpu.SemaphoreType.DMA((10,)),
            pltpu.SemaphoreType.DMA((10,)),
        ],
        compiler_params=pltpu.CompilerParams(vmem_limit_bytes=60 * 1024 * 1024),
    )(*results)


def shards(
    kv_cache, first_fresh, second_fresh, first_query, second_query, key_basis, out_weight,
    lengths, leave_slot, arrive_row,
):
    operands = (
        leave_slot.T, arrive_row.T, lengths.T, kv_cache[:, 0].transpose(0, 2, 1),
        first_fresh[:, 0], second_fresh[:, 0], first_query[:, 0], second_query[:, 0],
        key_basis[0], out_weight,
    )
    *results, fits = run_fast(*operands)
    out1, out2, cache = lax.cond(
        fits[0, 0] == 1,
        lambda: tuple(pass_straight(*results)),
        lambda: tuple(pass_on(*run_general(*operands))),
    )
    return out1, out2, cache.transpose(0, 2, 1)[:, None]


def solution(mesh):
    placed = (
        P("req", "head", None, None),
        P("req", "head", None),
        P("req", "head", None),
        P("req", "head", None),
        P("req", "head", None),
        P("head", None, None),
        P("head", None),
        P(),
        P(),
        P(),
    )
    return jax.shard_map(
        shards,
        mesh=mesh,
        in_specs=placed,
        out_specs=(P("req", "head"), P("req", "head"), P("req", "head", None, None)),
        check_vma=False,
    )
```
